512 devices in a mesh: sec: 2 (over core), dp: 64 (over x, z_hi, y), mp: 4 (over z_lo).
Axes of the slice: x: 4, y: 4, z: 16 (z_hi: 4, z_lo: 4; z = z_hi * 4 + z_lo), core: 2. Of those that a mesh axis runs over, the one named last changes fastest.
Arguments:
- states: bfloat16 [2, 32768, 896], P('sec', 'dp'), may hold values from -16 to 16
- proj_weights: bfloat16 [2, 896, 2, 2048], P('sec', None, None, 'mp'), may hold values from -0.1875 to 0.1875
- queries: bfloat16 [8192, 2048], P('dp', 'mp'), may hold values from -6 to 6
- out_grad: bfloat16 [8192, 2048], P('dp', 'mp'), may hold values from -24 to 24
- logsumexp: float32 [16, 8192], P('mp', 'dp'), may hold values from 3 to 5
- delta: float32 [16, 8192], P('mp', 'dp'), may hold values from -96 to 96
- span_blocks: int32 [128, 2], P('dp'), may hold values from 0 to 3, all different within a row
Outputs:
- row_grads: bfloat16 [2, 32768, 896], P('sec', ('dp', 'mp'))
- weight_grads: float32 [2, 896, 2, 2048], P('sec', 'dp', None, 'mp')
The draws below stay inside these ranges and needn't reach their ends.
Inputs may be any that keep to these rules, and one draw needn't show every extreme that they name: `span_blocks`: the two blocks of a span differ, and each block number occurs in some row.
All inputs are finite; a program needn't handle non-finite values.
Results may differ from the reference program's by a relative error of at most 0.022.
Values may be sent and summed in bfloat16 or wider, within the bound.
No kernel may reach another device: no remote copies, remote signals or barrier semaphores. Data moves between devices by JAX's collectives and lax.ppermute only.
A program may use at most 64 MiB of HBM per device.

```python
import jax
import jax.numpy as jnp
from jax import lax

ENC_D = 896
HEADS = 16
HEAD_DIM = 128
SPAN = 64
NEIGH_LEN = 128
CH_DEV = 2
ATT_W = 2048
SPANS = 128
TOKENS = 8192
ROWS = 32768
N_DP = 64
N_MP = 4


def strengthened(values, own_key, source, target, blocks, factor):
    owner, partner = [(jnp.arange(values.shape[axis_at]) // (values.shape[axis_at] // blocks)).reshape([-1 if axis == axis_at else 1 for axis in range(values.ndim)]) for axis_at in (source, target)]
    chosen = jax.random.permutation(own_key, blocks)[partner]
    strong = (owner == chosen) | (owner == (partner + blocks // 2) % blocks)
    return jnp.where(strong, factor * values, values)


def levels(stream_key, dims, shards, low, high):
    gain, own = 1.0, jax.random.fold_in(stream_key, 6)
    for axis_at, shards_of in shards:
        steps = jnp.exp(jax.random.uniform(jax.random.fold_in(own, axis_at), (shards_of,), jnp.float32, low / len(shards), high / len(shards)))
        gain = gain * jnp.repeat(steps, dims[axis_at] // shards_of).reshape([-1 if axis == axis_at else 1 for axis in range(len(dims))])
    return gain


def distinct(stream_key, rows, amount, top, lift):
    order = jax.random.permutation(jax.random.fold_in(stream_key, 1), amount)
    boost = order
    for power in range(3):
        boost = boost * boost // amount
    boost = boost * lift // amount
    tickets = jax.random.randint(jax.random.fold_in(stream_key, 2), (rows, amount), 0, 4096) + boost
    holders = jax.random.permutation(jax.random.fold_in(stream_key, 3), rows)[jnp.arange(amount) % rows]
    tickets = jnp.where(jnp.arange(rows)[:, None] == holders[None, :], 1 << 14, tickets)
    score = tickets * amount + jnp.arange(amount)
    return lax.top_k(score.astype(jnp.int32), top)[1].astype(jnp.int32)


def centred(rng, dims, width, bound, split=(), kind=jnp.bfloat16):
    values = jax.random.normal(rng, dims, jnp.float32) * width
    if len(split) > 0:
        values = levels(rng, dims, split, -0.22, 0.18) * values
    return jnp.clip(values, min=-bound, max=bound).astype(kind)


def heavy_noise(key, extent, spread, limit, split, heavy, kind=jnp.bfloat16):
    drawn = spread * jax.random.normal(key, extent, jnp.float32)
    if split:
        drawn = drawn * levels(key, extent, split, -0.22, 0.18)
    return jnp.clip(strengthened(drawn, jax.random.fold_in(key, 3), *heavy), -limit, limit).astype(kind)


def setup_inputs(seed: int = 0) -> dict:
    key_list = jax.random.split(jax.random.key(seed), 8)
    return {
        "states": heavy_noise(key_list[0], (2, ROWS, ENC_D), 1.0, 16.0, ((0, 2), (1, 64)), (1, 2, 64, 4.0)),
        "proj_weights": centred(key_list[1], (2, ENC_D, 2, ATT_W), ENC_D ** -0.5, 0.1875, ((0, 2), (3, 4))),
        "queries": centred(key_list[2], (TOKENS, ATT_W), 1.0, 6.0, ((0, 64), (1, 4))),
        "out_grad": centred(key_list[3], (TOKENS, ATT_W), 4.0, 24.0, ((0, 64), (1, 4))),
        "logsumexp": jnp.clip(3.0 + 2.0 * jax.random.uniform(key_list[4], (HEADS, TOKENS), jnp.float32) ** levels(key_list[4], (HEADS, TOKENS), ((0, 4), (1, 64)), -0.2, 0.2), 3.0, 5.0),
        "delta": centred(key_list[5], (HEADS, TOKENS), 16.0, 96.0, ((0, 4), (1, 64)), jnp.float32),
        "span_blocks": distinct(key_list[6], SPANS, 2 * CH_DEV, 2, 4096),
    }


def gelu_value(pre_act):
    inner = 0.7978845608 * (pre_act + 0.044715 * pre_act * pre_act * pre_act)
    return 0.5 * pre_act * (1.0 + jnp.tanh(inner))


def gelu_slope(pre_act):
    inner = 0.7978845608 * (pre_act + 0.044715 * pre_act * pre_act * pre_act)
    tangent = jnp.tanh(inner)
    return 0.5 * (1.0 + tangent) + 0.5 * pre_act * (1.0 - tangent * tangent) * 0.7978845608 * (1.0 + 0.134145 * pre_act * pre_act)


def part_sum(left_rows, right_weight):
    per_part = ATT_W // N_MP
    total = jnp.zeros((left_rows.shape[0], right_weight.shape[0]), jnp.float32)
    for part_index in range(N_MP):
        col_lo = part_index * per_part
        part_term = jnp.dot(left_rows[:, col_lo:col_lo + per_part], right_weight[:, col_lo:col_lo + per_part].T, preferred_element_type=jnp.float32)
        rounded = lax.optimization_barrier(part_term.astype(jnp.bfloat16))
        total = total + rounded.astype(jnp.float32)
    return total


def reference(states, proj_weights, queries, out_grad, logsumexp, delta, span_blocks):
    score_scale = HEAD_DIM ** -0.5
    blocks_all = 2 * CH_DEV * N_DP
    dec_rows = states[0]
    enc_in = states[1]
    key_weight = proj_weights[0, :, 0, :]
    value_weight = proj_weights[0, :, 1, :]
    up_weight = proj_weights[1, :, 0, :]
    down_weight_t = proj_weights[1, :, 1, :]
    key_rows = jnp.dot(dec_rows, key_weight, preferred_element_type=jnp.float32).astype(jnp.bfloat16)
    value_rows = jnp.dot(dec_rows, value_weight, preferred_element_type=jnp.float32).astype(jnp.bfloat16)
    groups = jnp.arange(SPANS, dtype=jnp.int32) // CH_DEV
    global_ids = (span_blocks + (groups * (2 * CH_DEV))[:, None]).astype(jnp.int32)
    key_slots = key_rows.reshape(blocks_all, NEIGH_LEN, HEADS, HEAD_DIM)[global_ids]
    key_slots = key_slots.reshape(SPANS, 2 * NEIGH_LEN, HEADS, HEAD_DIM).astype(jnp.float32)
    value_slots = value_rows.reshape(blocks_all, NEIGH_LEN, HEADS, HEAD_DIM)[global_ids]
    value_slots = value_slots.reshape(SPANS, 2 * NEIGH_LEN, HEADS, HEAD_DIM).astype(jnp.float32)
    query_rows = queries.reshape(SPANS, SPAN, HEADS, HEAD_DIM).astype(jnp.float32)
    grad_rows = out_grad.reshape(SPANS, SPAN, HEADS, HEAD_DIM).astype(jnp.float32)
    row_stats = logsumexp.reshape(HEADS, SPANS, SPAN).transpose(1, 0, 2)
    row_delta = delta.reshape(HEADS, SPANS, SPAN).transpose(1, 0, 2)
    scores = jnp.einsum('cqhd,ckhd->chqk', query_rows, key_slots) * score_scale
    attn_probs = jnp.exp(scores - row_stats[..., None])
    probs_low = attn_probs.astype(jnp.bfloat16).astype(jnp.float32)
    slot_vgrad = jnp.einsum('chqk,cqhd->ckhd', probs_low, grad_rows)
    grad_probs = jnp.einsum('cqhd,ckhd->chqk', grad_rows, value_slots)
    grad_scores = (attn_probs * (grad_probs - row_delta[..., None])).astype(jnp.bfloat16).astype(jnp.float32)
    slot_kgrad = score_scale * jnp.einsum('chqk,cqhd->ckhd', grad_scores, query_rows)
    flat_ids = global_ids.reshape(-1)
    block_keys = jax.ops.segment_sum(slot_kgrad.reshape(SPANS * 2, NEIGH_LEN * ATT_W), flat_ids, num_segments=blocks_all)
    block_keys = block_keys.astype(jnp.bfloat16).reshape(ROWS, ATT_W)
    block_values = jax.ops.segment_sum(slot_vgrad.reshape(SPANS * 2, NEIGH_LEN * ATT_W), flat_ids, num_segments=blocks_all)
    block_values = block_values.astype(jnp.bfloat16).reshape(ROWS, ATT_W)
    enc_sum = jnp.zeros((ROWS, ENC_D), jnp.float32)
    per_part = ATT_W // N_MP
    for part_index in range(N_MP):
        col_lo = part_index * per_part
        part_term = jnp.dot(block_keys[:, col_lo:col_lo + per_part], key_weight[:, col_lo:col_lo + per_part].T, preferred_element_type=jnp.float32)
        part_term = part_term + jnp.dot(block_values[:, col_lo:col_lo + per_part], value_weight[:, col_lo:col_lo + per_part].T, preferred_element_type=jnp.float32)
        rounded = lax.optimization_barrier(part_term.astype(jnp.bfloat16))
        enc_sum = enc_sum + rounded.astype(jnp.float32)
    enc_grads = enc_sum.astype(jnp.bfloat16)
    pre_act = jnp.dot(enc_in, up_weight, preferred_element_type=jnp.float32)
    hidden = gelu_value(pre_act).astype(jnp.bfloat16)
    grad_hidden = jnp.dot(enc_grads, down_weight_t, preferred_element_type=jnp.float32)
    grad_pre = (grad_hidden * gelu_slope(pre_act)).astype(jnp.bfloat16)
    input_grads = part_sum(grad_pre, up_weight).astype(jnp.bfloat16)
    dec_weights = jnp.stack([jnp.dot(dec_rows.T, block_keys, preferred_element_type=jnp.float32), jnp.dot(dec_rows.T, block_values, preferred_element_type=jnp.float32)], axis=1) / N_DP
    enc_weights = jnp.stack([jnp.dot(enc_in.T, grad_pre, preferred_element_type=jnp.float32), jnp.dot(enc_grads.T, hidden, preferred_element_type=jnp.float32)], axis=1) / N_DP
    return jnp.stack([enc_grads, input_grads]), jnp.stack([dec_weights, enc_weights])
```

```python
import jax
import jax.numpy as jnp
from jax import lax
from jax.experimental import pallas as pl
from jax.experimental.pallas import tpu as pltpu
from jax.sharding import Mesh
from jax.sharding import PartitionSpec as P

HEAD_DIM = 128
SPAN = 64
NEIGH = 128
BLOCKS = 4
N_MP = 4
SIDE = 4
SCALE = HEAD_DIM ** (-0.5)
F32 = jnp.float32
BF16 = jnp.bfloat16
NT = (((1,), (1,)), ((), ()))
TN = (((0,), (0,)), ((), ()))
VMEM_LIMIT = 48 * 1024 * 1024


def mm(left, right, dims=(((1,), (0,)), ((), ()))):
    return lax.dot_general(left, right, dims, preferred_element_type=F32)


def block_rows(index):
    return pl.ds(pl.multiple_of(index * NEIGH, NEIGH), NEIGH)


def decoder_kernel(mp_ref, span_ref, rows_ref, weight_ref, query_ref, grad_ref, lse_ref, delta_ref,
                   kv_grad_ref, part0, part1, part2, part3, kv_ref):
    half = weight_ref.shape[1] // 2
    kv_ref[...] = mm(rows_ref[...], weight_ref[...]).astype(BF16)
    lane = lax.broadcasted_iota(jnp.int32, (1, 2 * SPAN), 1)
    used = []
    for block in range(BLOCKS):
        flags = [
            jnp.where((span_ref[c, 0] == block) | (span_ref[c, 1] == block), 1, 0) for c in range(2)
        ]
        used.append(jnp.where(lane < SPAN, flags[0], flags[1]) > 0)
    for head in range(half // HEAD_DIM):
        lo = head * HEAD_DIM
        query = query_ref[:, lo:lo + HEAD_DIM]
        grad = grad_ref[:, lo:lo + HEAD_DIM]
        lse = lse_ref[head:head + 1, :]
        delta = delta_ref[head:head + 1, :]
        for block in range(BLOCKS):
            r0 = block * NEIGH
            key = kv_ref[r0:r0 + NEIGH, lo:lo + HEAD_DIM]
            value = kv_ref[r0:r0 + NEIGH, half + lo:half + lo + HEAD_DIM]
            shift = jnp.where(used[block], lse, jnp.inf)
            probs = jnp.exp(mm(key, query, NT) * SCALE - shift)
            value_grad = mm(probs.astype(BF16), grad)
            score_grad = probs * (mm(value, grad, NT) - delta)
            key_grad = mm(score_grad.astype(BF16), query) * SCALE
            kv_grad_ref[r0:r0 + NEIGH, lo:lo + HEAD_DIM] = key_grad.astype(BF16)
            kv_grad_ref[r0:r0 + NEIGH, half + lo:half + lo + HEAD_DIM] = value_grad.astype(BF16)
    mp = mp_ref[0]
    for step, part in enumerate((part0, part1, part2, part3)):
        rows = kv_grad_ref[block_rows(lax.rem(mp + step, N_MP)), :]
        part[...] = mm(rows, weight_ref[...], NT).astype(BF16)


def prepare_kernel(rows_ref, weight_ref, hidden_ref, slope_ref):
    half = weight_ref.shape[1] // 2
    pre = mm(rows_ref[...], weight_ref[:, :half])
    square = pre * pre
    tangent = jnp.tanh(0.7978845608 * (pre + 0.044715 * square * pre))
    hidden_ref[...] = (0.5 * pre * (1.0 + tangent)).astype(BF16)
    slope_ref[...] = 0.5 * (1.0 + tangent) + 0.5 * pre * (1.0 - tangent * tangent) * 0.7978845608 * (
        1.0 + 0.134145 * square
    )


def encoder_kernel(mp_ref, rows_ref, weight_ref, hidden_ref, slope_ref, got0, got1, got2, got3,
                   partial_ref, part0, part1, part2, part3, pre_grad_ref, arrived_ref):
    half = weight_ref.shape[1] // 2
    mp = mp_ref[0]
    up = weight_ref[:, :half]
    for step, (got, part) in enumerate(zip((got0, got3, got2, got1), (part0, part1, part2, part3))):
        rows = block_rows(lax.rem(mp + step, N_MP))
        arrived_ref[rows, :] = got[...]
        hidden_grad = mm(got[...], weight_ref[:, half:])
        pre_grad = (hidden_grad * slope_ref[rows, :]).astype(BF16)
        pre_grad_ref[rows, :] = pre_grad
        part[...] = mm(pre_grad, up, NT).astype(BF16)
    partial_ref[:, half:] = mm(arrived_ref[...], hidden_ref[...], TN).astype(BF16)
    partial_ref[:, :half] = mm(rows_ref[...], pre_grad_ref[...], TN).astype(BF16)


def weight_kernel(rows_ref, kv_grad_ref, partial_ref):
    partial_ref[...] = mm(rows_ref[...], kv_grad_ref[...], TN).astype(BF16)


def sum_kernel(piece_ref, out0, out1, out2, out3, total_ref):
    total = piece_ref[0].astype(F32)
    for source in range(1, piece_ref.shape[0]):
        total = total + piece_ref[source].astype(F32)
    count = total.shape[0]
    share = count // SIDE
    total_ref[:count, :] = total
    total_ref[count:, :] = jnp.zeros((total_ref.shape[0] - count, total_ref.shape[1]), F32)
    for index, out in enumerate((out0, out1, out2, out3)):
        first = index * share
        out[...] = total_ref[first:first + out.shape[0], :].astype(BF16)


def vmem():
    return pl.BlockSpec(memory_space=pltpu.VMEM)


def smem():
    return pl.BlockSpec(memory_space=pltpu.SMEM)


def call(kernel, outs, args, scalars=0, scratch=(), flops=0):
    return pl.pallas_call(
        kernel,
        out_shape=[jax.ShapeDtypeStruct(shape, kind) for shape, kind in outs],
        in_specs=[smem()] * scalars + [vmem()] * (len(args) - scalars),
        out_specs=[vmem()] * len(outs),
        scratch_shapes=list(scratch),
        compiler_params=pltpu.CompilerParams(vmem_limit_bytes=VMEM_LIMIT),
        cost_estimate=pl.CostEstimate(flops=flops, bytes_accessed=4 << 20, transcendentals=0),
    )(*args)


def mp_move(value, source, target, step):
    pairs = [(source * N_MP + m, target * N_MP + (m + step) % N_MP) for m in range(N_MP)]
    return lax.ppermute(value, ("sec", "mp"), pairs)


def mp_sum(parts, section):
    total = parts[0].astype(F32)
    for step in (2, 1, 3):
        total = total + mp_move(parts[step], section, section, step).astype(F32)
    return total.astype(BF16)


def shards(states, proj_weights, queries, out_grad, logsumexp, delta, span_blocks):
    rows = states[0]
    local_rows, width = rows.shape
    half = proj_weights.shape[3]
    weights = proj_weights[0].reshape(width, 2 * half)
    quarter = local_rows // N_MP
    is_decoder = lax.axis_index("sec") == 0
    mp = lax.axis_index("mp").astype(jnp.int32).reshape(1)
    part_outs = [((quarter, width), BF16)] * N_MP

    def decoder_branch():
        kv_grad, *parts = call(
            decoder_kernel,
            [((local_rows, 2 * half), BF16)] + part_outs,
            (mp, span_blocks, rows, weights, queries, out_grad, logsumexp, delta),
            scalars=2,
            scratch=[pltpu.VMEM((local_rows, 2 * half), BF16)],
            flops=4 * local_rows * width * 2 * half,
        )
        return (kv_grad, jnp.zeros((local_rows, half), F32), *parts)

    def prepare_branch():
        hidden, slope = call(
            prepare_kernel,
            [((local_rows, half), BF16), ((local_rows, half), F32)],
            (rows, weights),
            flops=2 * local_rows * width * half,
        )
        empty = jnp.zeros((quarter, width), BF16)
        return (jnp.concatenate([hidden, hidden], axis=1), slope, empty, empty, empty, empty)

    mixed, slope, *enc_parts = lax.cond(is_decoder, decoder_branch, prepare_branch)
    enc_share = mp_sum(enc_parts, 0)
    got = [mp_move(enc_share, 0, 1, step) for step in range(N_MP)]

    def decoder_weights():
        (partial,) = call(
            weight_kernel, [((width, 2 * half), BF16)], (rows, mixed), flops=4 * local_rows * width * half
        )
        empty = jnp.zeros((quarter, width), BF16)
        return (partial, empty, empty, empty, empty)

    def encoder_branch():
        return tuple(
            call(
                encoder_kernel,
                [((width, 2 * half), BF16)] + part_outs,
                (mp, rows, weights, mixed[:, :half], slope, *got),
                scalars=1,
                scratch=[pltpu.VMEM((local_rows, half), BF16), pltpu.VMEM((local_rows, width), BF16)],
                flops=8 * local_rows * width * half,
            )
        )

    partial, *in_parts = lax.cond(is_decoder, decoder_weights, encoder_branch)
    in_share = mp_sum(in_parts, 1)
    pieces = lax.all_to_all(partial, ("x", "y"), 0, 0, tiled=True)
    chunk = width // (SIDE * SIDE)
    padded = 16
    blocks = call(
        sum_kernel,
        [((padded, 2 * half), BF16)] * SIDE,
        (pieces.reshape(SIDE * SIDE, chunk, 2 * half),),
        scratch=[pltpu.VMEM((SIDE * padded, 2 * half), F32)],
    )
    zh = lax.axis_index("zh")
    total = jnp.zeros((padded, 2 * half), F32)
    for step in range(SIDE):
        target = lax.rem(zh + step, SIDE)
        block = blocks[0]
        for index in range(1, SIDE):
            block = jnp.where(target == index, blocks[index], block)
        pairs = [
            (b * SIDE + a, a * SIDE + (b + step) % SIDE) for b in range(SIDE) for a in range(SIDE)
        ]
        total = total + lax.ppermute(block, ("zh", "y"), pairs).astype(F32)
    share = chunk // SIDE
    weight_part = (total[:share] / (SIDE * SIDE * SIDE)).reshape(1, share, 2, half)
    return (jnp.where(is_decoder, enc_share, in_share)[None], weight_part)


def solution(mesh):
    split = Mesh(mesh.devices.reshape(2, SIDE, SIDE, SIDE, N_MP), ("sec", "x", "zh", "y", "mp"))
    dp = ("x", "zh", "y")
    in_specs = (
        P("sec", dp, None),
        P("sec", None, None, "mp"),
        P(dp, "mp"),
        P(dp, "mp"),
        P("mp", dp),
        P("mp", dp),
        P(dp, None),
    )
    out_specs = (P("sec", (*dp, "mp"), None), P("sec", dp, None, "mp"))
    return jax.shard_map(shards, mesh=split, in_specs=in_specs, out_specs=out_specs, check_vma=False)
```

```python
import jax
import jax.numpy as jnp
from jax import lax
from jax.experimental import pallas as pl
from jax.experimental.pallas import tpu as pltpu
from jax.sharding import Mesh
from jax.sharding import PartitionSpec as P

HEAD_DIM = 128
SPAN = 64
NEIGH = 128
BLOCKS = 4
N_MP = 4
SIDE = 4
PADDED = 16
SCALE = HEAD_DIM ** (-0.5)
F32 = jnp.float32
BF16 = jnp.bfloat16
NT = (((1,), (1,)), ((), ()))
TN = (((0,), (0,)), ((), ()))
VMEM_LIMIT = 48 * 1024 * 1024


def mm(left, right, dims=(((1,), (0,)), ((), ()))):
    return lax.dot_general(left, right, dims, preferred_element_type=F32)


def block_rows(index):
    return pl.ds(pl.multiple_of(index * NEIGH, NEIGH), NEIGH)


def on_section(sec_ref, section):
    return pl.when(sec_ref[0] == section)


def decoder_kernel(mp_ref, span_ref, rows_ref, weight_ref, query_ref, grad_ref, lse_ref, delta_ref,
                   kv_grad_ref, part0, part1, part2, part3, kv_ref, part_ref):
    half = weight_ref.shape[1] // 2
    kv_ref[...] = mm(rows_ref[...], weight_ref[...]).astype(BF16)
    lane = lax.broadcasted_iota(jnp.int32, (1, 2 * SPAN), 1)
    used = []
    for block in range(BLOCKS):
        flags = [
            jnp.where((span_ref[c, 0] == block) | (span_ref[c, 1] == block), 1, 0) for c in range(2)
        ]
        used.append(jnp.where(lane < SPAN, flags[0], flags[1]) > 0)
    for head in range(half // HEAD_DIM):
        lo = head * HEAD_DIM
        query = query_ref[:, lo:lo + HEAD_DIM]
        grad = grad_ref[:, lo:lo + HEAD_DIM]
        lse = lse_ref[head:head + 1, :]
        delta = delta_ref[head:head + 1, :]
        key = kv_ref[:, lo:lo + HEAD_DIM]
        value = kv_ref[:, half + lo:half + lo + HEAD_DIM]
        shift = jnp.concatenate(
            [jnp.broadcast_to(jnp.where(flag, lse, jnp.inf), (NEIGH, 2 * SPAN)) for flag in used], axis=0
        )
        probs = jnp.exp(mm(key, query, NT) * SCALE - shift)
        value_grad = mm(probs.astype(BF16), grad)
        score_grad = probs * (mm(value, grad, NT) - delta)
        key_grad = mm(score_grad.astype(BF16), query) * SCALE
        kv_grad_ref[:, lo:lo + HEAD_DIM] = key_grad.astype(BF16)
        kv_grad_ref[:, half + lo:half + lo + HEAD_DIM] = value_grad.astype(BF16)
    part_ref[...] = mm(kv_grad_ref[...], weight_ref[...], NT).astype(BF16)
    for step, part in enumerate((part0, part1, part2, part3)):
        part[...] = part_ref[block_rows(lax.rem(mp_ref[0] + step, N_MP)), :]


def ordered(rows, order_ref):
    width = order_ref.shape[1]
    place = lax.broadcasted_iota(jnp.int32, (width, width), 0) == order_ref[...]
    return mm(rows, jnp.where(place, 1.0, 0.0).astype(BF16)).astype(BF16)


def store_chunks(out_ref, value):
    chunk = out_ref.shape[1]
    for index in range(out_ref.shape[0]):
        out_ref[index] = value[index * chunk:(index + 1) * chunk, :].astype(BF16)


def decoder_weight_kernel(sec_ref, rows_ref, kv_grad_ref, order_ref, first_ref, second_ref):
    @on_section(sec_ref, 0)
    def work():
        half = kv_grad_ref.shape[1] // 2
        rows = ordered(rows_ref[...], order_ref)
        store_chunks(second_ref, mm(rows, kv_grad_ref[:, half:], TN))
        store_chunks(first_ref, mm(rows, kv_grad_ref[:, :half], TN))


def prepare_kernel(rows_ref, weight_ref, order_ref, ordered_ref, hidden_ref, slope_ref):
    half = weight_ref.shape[1] // 2
    ordered_ref[...] = ordered(rows_ref[...], order_ref)
    pre = mm(rows_ref[...], weight_ref[:, :half])
    square = pre * pre
    tangent = jnp.tanh(0.7978845608 * (pre + 0.044715 * square * pre))
    hidden_ref[...] = (0.5 * pre * (1.0 + tangent)).astype(BF16)
    slope_ref[...] = 0.5 * (1.0 + tangent) + 0.5 * pre * (1.0 - tangent * tangent) * 0.7978845608 * (
        1.0 + 0.134145 * square
    )


def first_kernel(sec_ref, mp_ref, span_ref, rows_ref, weight_ref, query_ref, grad_ref, lse_ref, delta_ref, order_ref,
                 kv_grad_ref, part0, part1, part2, part3, ordered_ref, hidden_ref, slope_ref, kv_ref, part_ref):
    @on_section(sec_ref, 0)
    def decoder():
        decoder_kernel(
            mp_ref, span_ref, rows_ref, weight_ref, query_ref, grad_ref, lse_ref, delta_ref,
            kv_grad_ref, part0, part1, part2, part3, kv_ref, part_ref,
        )

    @on_section(sec_ref, 1)
    def encoder():
        prepare_kernel(rows_ref, weight_ref, order_ref, ordered_ref, hidden_ref, slope_ref)


def down_kernel(sec_ref, mp_ref, order_ref, hidden_ref, got0, got1, got2, got3, arrived_ref, second_ref):
    @on_section(sec_ref, 1)
    def work():
        for step, got in enumerate((got0, got3, got2, got1)):
            arrived_ref[block_rows(lax.rem(mp_ref[0] + step, N_MP)), :] = got[...]
        store_chunks(second_ref, mm(ordered(arrived_ref[...], order_ref), hidden_ref[...], TN))


def up_kernel(sec_ref, mp_ref, ordered_ref, weight_ref, slope_ref, arrived_ref, first_ref, part0, part1, part2, part3,
              part_ref):
    @on_section(sec_ref, 1)
    def work():
        half = weight_ref.shape[1] // 2
        hidden_grad = mm(arrived_ref[...], weight_ref[:, half:])
        pre_grad = (hidden_grad * slope_ref[...]).astype(BF16)
        store_chunks(first_ref, mm(ordered_ref[...], pre_grad, TN))
        part_ref[...] = mm(pre_grad, weight_ref[:, :half], NT).astype(BF16)
        for step, part in enumerate((part0, part1, part2, part3)):
            part[...] = part_ref[block_rows(lax.rem(mp_ref[0] + step, N_MP)), :]


def chunk_sum(piece_ref, total_ref):
    total = piece_ref[0].astype(F32)
    for source in range(1, piece_ref.shape[0]):
        total = total + piece_ref[source].astype(F32)
    count = total.shape[0]
    share = count // SIDE
    total_ref[:count, :] = total
    total_ref[count:, :] = jnp.zeros((total_ref.shape[0] - count, total_ref.shape[1]), F32)
    return jnp.concatenate(
        [total_ref[index * share:index * share + PADDED, :] for index in range(SIDE)], axis=0
    ).astype(BF16)


def early_sum_kernel(piece_ref, out_ref, total_ref):
    out_ref[...] = chunk_sum(piece_ref, total_ref)


def late_sum_kernel(sec_ref, piece_ref, early_ref, own_ref, other_ref, total_ref):
    late = chunk_sum(piece_ref, total_ref)

    @pl.when(sec_ref[0] == 0)
    def decoder():
        own_ref[...] = early_ref[...]
        other_ref[...] = late

    @pl.when(sec_ref[0] != 0)
    def encoder():
        own_ref[...] = late
        other_ref[...] = early_ref[...]


def join_kernel(zh_ref, own_ref, came_ref, out0, out1, out2, out3):
    half = own_ref.shape[1]
    for step, out in enumerate((out0, out1, out2, out3)):
        rows = pl.ds(pl.multiple_of(lax.rem(zh_ref[0] + step, SIDE) * PADDED, PADDED), PADDED)
        out[:, :half] = own_ref[rows, :]
        out[:, half:] = came_ref[rows, :]


def vmem():
    return pl.BlockSpec(memory_space=pltpu.VMEM)


def smem():
    return pl.BlockSpec(memory_space=pltpu.SMEM)


def call(kernel, outs, args, scalars=0, scratch=(), flops=0):
    return pl.pallas_call(
        kernel,
        out_shape=[jax.ShapeDtypeStruct(shape, kind) for shape, kind in outs],
        in_specs=[smem()] * scalars + [vmem()] * (len(args) - scalars),
        out_specs=[vmem()] * len(outs),
        scratch_shapes=list(scratch),
        compiler_params=pltpu.CompilerParams(vmem_limit_bytes=VMEM_LIMIT),
        cost_estimate=pl.CostEstimate(flops=flops, bytes_accessed=4 << 20, transcendentals=0),
    )(*args)


def mp_move(value, source, target, step):
    pairs = [(source * N_MP + m, target * N_MP + (m + step) % N_MP) for m in range(N_MP)]
    return lax.ppermute(value, ("sec", "mp"), pairs)


def mp_sum(parts, section):
    total = parts[0].astype(F32)
    for step in (2, 1, 3):
        total = total + mp_move(parts[step], section, section, step).astype(F32)
    return total.astype(BF16)


def shards(states, proj_weights, queries, out_grad, logsumexp, delta, span_blocks):
    rows = states[0]
    local_rows, width = rows.shape
    half = proj_weights.shape[3]
    weights = proj_weights[0].reshape(width, 2 * half)
    quarter = local_rows // N_MP
    pieces = SIDE * SIDE
    chunk = width // pieces
    share = chunk // SIDE
    sec = lax.axis_index("sec").astype(jnp.int32).reshape(1)
    mp = lax.axis_index("mp").astype(jnp.int32).reshape(1)
    zh = lax.axis_index("zh").astype(jnp.int32).reshape(1)
    is_decoder = sec[0] == 0
    order = jnp.arange(width, dtype=jnp.int32).reshape(SIDE, SIDE, SIDE, share)
    order = order.transpose(0, 2, 1, 3).reshape(1, width)

    part_outs = [((quarter, width), BF16)] * N_MP
    piece_out = ((pieces, chunk, half), BF16)
    col_out = ((local_rows, half), BF16)
    sum_out = ((SIDE * PADDED, half), BF16)
    part_scratch = pltpu.VMEM((local_rows, width), BF16)
    sum_scratch = pltpu.VMEM((SIDE * PADDED, half), F32)
    cols_flops = 2 * local_rows * width * half

    ordered_out = ((local_rows, width), BF16)
    kv_grad, *enc_parts, ordered_rows, hidden, slope = call(
        first_kernel,
        [((local_rows, 2 * half), BF16)] + part_outs + [ordered_out, col_out, ((local_rows, half), F32)],
        (sec, mp, span_blocks, rows, weights, queries, out_grad, logsumexp, delta, order),
        scalars=3,
        scratch=[pltpu.VMEM((local_rows, 2 * half), BF16), part_scratch],
        flops=4 * cols_flops,
    )
    enc_share = mp_sum(enc_parts, 0)
    got = [mp_move(enc_share, 0, 1, step) for step in range(N_MP)]

    first, second = call(
        decoder_weight_kernel, [piece_out] * 2, (sec, rows, kv_grad, order), scalars=1, flops=4 * cols_flops
    )
    second = lax.ppermute(second, "sec", [(0, 1)])
    early = lax.all_to_all(jnp.where(is_decoder, first, second), ("x", "y"), 0, 0, tiled=True)
    (early_sum,) = call(early_sum_kernel, [sum_out], (early,), scratch=[sum_scratch])
    early_sum, *got = lax.optimization_barrier((early_sum, *got))

    arrived, down = call(
        down_kernel, [ordered_out, piece_out], (sec, mp, order, hidden, *got), scalars=2, flops=3 * cols_flops
    )
    down = lax.ppermute(down, "sec", [(1, 0)])
    up, *in_parts = call(
        up_kernel,
        [piece_out] + part_outs,
        (sec, mp, ordered_rows, weights, slope, arrived),
        scalars=2,
        scratch=[part_scratch],
        flops=3 * cols_flops,
    )
    in_share = mp_sum(in_parts, 1)
    late = lax.all_to_all(jnp.where(is_decoder, down, up), ("x", "y"), 0, 0, tiled=True)
    own, other = call(late_sum_kernel, [sum_out] * 2, (sec, late, early_sum), scalars=1, scratch=[sum_scratch])
    came = lax.ppermute(other, "sec", [(0, 1), (1, 0)])
    blocks = call(join_kernel, [((PADDED, 2 * half), BF16)] * SIDE, (zh, own, came), scalars=1)
    total = blocks[0].astype(F32)
    for step in range(1, SIDE):
        pairs = [(source, (source + step) % SIDE) for source in range(SIDE)]
        total = total + lax.ppermute(blocks[step], "zh", pairs).astype(F32)
    weight_part = (total[:share] / (SIDE * SIDE * SIDE)).reshape(1, share, 2, half)
    return (jnp.where(is_decoder, enc_share, in_share)[None], weight_part)


def solution(mesh):
    split = Mesh(mesh.devices.reshape(2, SIDE, SIDE, SIDE, N_MP), ("sec", "x", "zh", "y", "mp"))
    dp = ("x", "zh", "y")
    in_specs = (
        P("sec", dp, None),
        P("sec", None, None, "mp"),
        P(dp, "mp"),
        P(dp, "mp"),
        P("mp", dp),
        P("mp", dp),
        P(dp, None),
    )
    out_specs = (P("sec", (*dp, "mp"), None), P("sec", dp, None, "mp"))
    return jax.shard_map(shards, mesh=split, in_specs=in_specs, out_specs=out_specs, check_vma=False)
```

```python
import jax
import jax.numpy as jnp
from jax import lax
from jax.experimental import pallas as pl
from jax.experimental.pallas import tpu as pltpu
from jax.sharding import Mesh
from jax.sharding import PartitionSpec as P

HEAD_DIM = 128
SPAN = 64
NEIGH = 128
BLOCKS = 4
N_MP = 4
SIDE = 4
PADDED = 16
SCALE = HEAD_DIM ** (-0.5)
F32 = jnp.float32
BF16 = jnp.bfloat16
NT = (((1,), (1,)), ((), ()))
TN = (((0,), (0,)), ((), ()))
VMEM_LIMIT = 12 * 1024 * 1024


def mm(left, right, dims=(((1,), (0,)), ((), ()))):
    return lax.dot_general(left, right, dims, preferred_element_type=F32)


def block_rows(index):
    return pl.ds(pl.multiple_of(index * NEIGH, NEIGH), NEIGH)


def on_section(sec_ref, section):
    return pl.when(sec_ref[0] == section)


def decoder_kernel(mp_ref, span_ref, rows_ref, weight_ref, query_ref, grad_ref, lse_ref, delta_ref,
                   kv_grad_ref, part0, part1, part2, part3, kv_ref, part_ref):
    half = weight_ref.shape[1] // 2
    kv_ref[...] = mm(rows_ref[...], weight_ref[...]).astype(BF16)
    lane = lax.broadcasted_iota(jnp.int32, (1, 2 * SPAN), 1)
    used = []
    for block in range(BLOCKS):
        flags = [
            jnp.where((span_ref[c, 0] == block) | (span_ref[c, 1] == block), 1, 0) for c in range(2)
        ]
        used.append(jnp.where(lane < SPAN, flags[0], flags[1]) > 0)
    for head in range(half // HEAD_DIM):
        lo = head * HEAD_DIM
        query = query_ref[:, lo:lo + HEAD_DIM]
        grad = grad_ref[:, lo:lo + HEAD_DIM]
        lse = lse_ref[head:head + 1, :]
        delta = delta_ref[head:head + 1, :]
        key = kv_ref[:, lo:lo + HEAD_DIM]
        value = kv_ref[:, half + lo:half + lo + HEAD_DIM]
        shift = jnp.concatenate(
            [jnp.broadcast_to(jnp.where(flag, lse, jnp.inf), (NEIGH, 2 * SPAN)) for flag in used], axis=0
        )
        probs = jnp.exp(mm(key, query, NT) * SCALE - shift)
        value_grad = mm(probs.astype(BF16), grad)
        score_grad = probs * (mm(value, grad, NT) - delta)
        key_grad = mm(score_grad.astype(BF16), query) * SCALE
        kv_grad_ref[:, lo:lo + HEAD_DIM] = key_grad.astype(BF16)
        kv_grad_ref[:, half + lo:half + lo + HEAD_DIM] = value_grad.astype(BF16)
    part_ref[...] = mm(kv_grad_ref[...], weight_ref[...], NT).astype(BF16)
    for step, part in enumerate((part0, part1, part2, part3)):
        part[...] = part_ref[block_rows(lax.rem(mp_ref[0] + step, N_MP)), :]


def ordered(rows, order_ref):
    width = order_ref.shape[1]
    place = lax.broadcasted_iota(jnp.int32, (width, width), 0) == order_ref[...]
    return mm(rows, jnp.where(place, 1.0, 0.0).astype(BF16)).astype(BF16)


def store_chunks(out_ref, value, column=0):
    chunk, width = out_ref.shape[1], value.shape[1]
    for index in range(out_ref.shape[0]):
        out_ref[index, :, column:column + width] = value[index * chunk:(index + 1) * chunk, :].astype(BF16)


def decoder_weight_kernel(sec_ref, rows_ref, kv_grad_ref, order_ref, partial_ref):
    @on_section(sec_ref, 0)
    def work():
        store_chunks(partial_ref, mm(ordered(rows_ref[...], order_ref), kv_grad_ref[...], TN))


def prepare_kernel(rows_ref, weight_ref, order_ref, ordered_ref, hidden_ref, slope_ref):
    half = weight_ref.shape[1] // 2
    ordered_ref[...] = ordered(rows_ref[...], order_ref)
    pre = mm(rows_ref[...], weight_ref[:, :half])
    square = pre * pre
    tangent = jnp.tanh(0.7978845608 * (pre + 0.044715 * square * pre))
    hidden_ref[...] = (0.5 * pre * (1.0 + tangent)).astype(BF16)
    slope_ref[...] = 0.5 * (1.0 + tangent) + 0.5 * pre * (1.0 - tangent * tangent) * 0.7978845608 * (
        1.0 + 0.134145 * square
    )


def first_kernel(sec_ref, mp_ref, span_ref, rows_ref, weight_ref, query_ref, grad_ref, lse_ref, delta_ref, order_ref,
                 kv_grad_ref, part0, part1, part2, part3, ordered_ref, hidden_ref, slope_ref, kv_ref, part_ref):
    @on_section(sec_ref, 0)
    def decoder():
        decoder_kernel(
            mp_ref, span_ref, rows_ref, weight_ref, query_ref, grad_ref, lse_ref, delta_ref,
            kv_grad_ref, part0, part1, part2, part3, kv_ref, part_ref,
        )

    @on_section(sec_ref, 1)
    def encoder():
        prepare_kernel(rows_ref, weight_ref, order_ref, ordered_ref, hidden_ref, slope_ref)


def encoder_kernel(sec_ref, mp_ref, order_ref, ordered_ref, weight_ref, hidden_ref, slope_ref, got0, got1, got2, got3,
                   keep_ref, partial_ref, part0, part1, part2, part3, arrived_ref, part_ref):
    del keep_ref
    @on_section(sec_ref, 1)
    def work():
        half = weight_ref.shape[1] // 2
        for step, got in enumerate((got0, got3, got2, got1)):
            arrived_ref[block_rows(lax.rem(mp_ref[0] + step, N_MP)), :] = got[...]
        arrived = arrived_ref[...]
        pre_grad = (mm(arrived, weight_ref[:, half:]) * slope_ref[...]).astype(BF16)
        store_chunks(partial_ref, mm(ordered(arrived, order_ref), hidden_ref[...], TN), half)
        store_chunks(partial_ref, mm(ordered_ref[...], pre_grad, TN))
        part_ref[...] = mm(pre_grad, weight_ref[:, :half], NT).astype(BF16)
        for step, part in enumerate((part0, part1, part2, part3)):
            part[...] = part_ref[block_rows(lax.rem(mp_ref[0] + step, N_MP)), :]


def sum_kernel(zh_ref, piece_ref, out0, out1, out2, out3, total_ref):
    total = piece_ref[0].astype(F32)
    for source in range(1, piece_ref.shape[0]):
        total = total + piece_ref[source].astype(F32)
    count = total.shape[0]
    share = count // SIDE
    total_ref[:count, :] = total
    total_ref[count:, :] = jnp.zeros((total_ref.shape[0] - count, total_ref.shape[1]), F32)
    for block in range(SIDE):
        rows = total_ref[block * share:block * share + PADDED, :].astype(BF16)
        for step, out in enumerate((out0, out1, out2, out3)):
            @pl.when(lax.rem(zh_ref[0] + step, SIDE) == block)
            def store(rows=rows, out=out):
                out[...] = rows


def vmem():
    return pl.BlockSpec(memory_space=pltpu.VMEM)


def smem():
    return pl.BlockSpec(memory_space=pltpu.SMEM)


def call(kernel, outs, args, scalars=0, scratch=(), flops=0, alias=None):
    return pl.pallas_call(
        kernel,
        out_shape=[jax.ShapeDtypeStruct(shape, kind) for shape, kind in outs],
        in_specs=[smem()] * scalars + [vmem()] * (len(args) - scalars),
        out_specs=[vmem()] * len(outs),
        scratch_shapes=list(scratch),
        input_output_aliases=alias or {},
        compiler_params=pltpu.CompilerParams(vmem_limit_bytes=VMEM_LIMIT),
        cost_estimate=pl.CostEstimate(flops=flops, bytes_accessed=4 << 20, transcendentals=0),
    )(*args)


def mp_move(value, source, target, step):
    pairs = [(source * N_MP + m, target * N_MP + (m + step) % N_MP) for m in range(N_MP)]
    return lax.ppermute(value, ("sec", "mp"), pairs)


def mp_parts(parts, section):
    return [parts[0]] + [mp_move(parts[step], section, section, step) for step in (2, 1, 3)]


def mp_sum(parts):
    total = parts[0].astype(F32)
    for part in parts[1:]:
        total = total + part.astype(F32)
    return total.astype(BF16)


def shards(states, proj_weights, queries, out_grad, logsumexp, delta, span_blocks):
    rows = states[0]
    local_rows, width = rows.shape
    half = proj_weights.shape[3]
    weights = proj_weights[0].reshape(width, 2 * half)
    quarter = local_rows // N_MP
    pieces = SIDE * SIDE
    chunk = width // pieces
    share = chunk // SIDE
    sec = lax.axis_index("sec").astype(jnp.int32).reshape(1)
    mp = lax.axis_index("mp").astype(jnp.int32).reshape(1)
    zh = lax.axis_index("zh").astype(jnp.int32).reshape(1)
    is_decoder = sec[0] == 0
    order = jnp.arange(width, dtype=jnp.int32).reshape(SIDE, SIDE, SIDE, share)
    order = order.transpose(0, 2, 1, 3).reshape(1, width)

    part_outs = [((quarter, width), BF16)] * N_MP
    piece_out = ((pieces, chunk, 2 * half), BF16)
    col_out = ((local_rows, half), BF16)
    part_scratch = pltpu.VMEM((local_rows, width), BF16)
    sum_scratch = pltpu.VMEM((SIDE * PADDED, 2 * half), F32)
    cols_flops = 2 * local_rows * width * half

    ordered_out = ((local_rows, width), BF16)
    kv_grad, *enc_parts, ordered_rows, hidden, slope = call(
        first_kernel,
        [((local_rows, 2 * half), BF16)] + part_outs + [ordered_out, col_out, ((local_rows, half), F32)],
        (sec, mp, span_blocks, rows, weights, queries, out_grad, logsumexp, delta, order),
        scalars=3,
        scratch=[pltpu.VMEM((local_rows, 2 * half), BF16), part_scratch],
        flops=4 * cols_flops,
    )
    with jax.named_scope("enc_reduce"):
        enc_parts = mp_parts(enc_parts, 0)
    enc_share = mp_sum(enc_parts)
    with jax.named_scope("enc_gather"):
        got = [mp_move(enc_share, 0, 1, step) for step in (2, 1, 3, 0)]
        got = [got[3], got[1], got[0], got[2]]

    (partial,) = call(
        decoder_weight_kernel, [piece_out], (sec, rows, kv_grad, order), scalars=1, flops=4 * cols_flops
    )
    partial, *in_parts = call(
        encoder_kernel,
        [piece_out] + part_outs,
        (sec, mp, order, ordered_rows, weights, hidden, slope, *got, partial),
        scalars=2,
        scratch=[part_scratch] * 2,
        flops=5 * cols_flops,
        alias={11: 0},
    )
    with jax.named_scope("exchange"):
        partial = lax.all_to_all(partial, ("x", "y"), 0, 0, tiled=True)
    with jax.named_scope("in_reduce"):
        in_parts = mp_parts(in_parts, 1)
    in_share = mp_sum(in_parts)
    blocks = call(
        sum_kernel, [((PADDED, 2 * half), BF16)] * SIDE, (zh, partial), scalars=1, scratch=[sum_scratch]
    )
    total = blocks[0].astype(F32)
    for step in range(1, SIDE):
        pairs = [(source, (source + step) % SIDE) for source in range(SIDE)]
        with jax.named_scope("zh_reduce"):
            came = lax.ppermute(blocks[step], "zh", pairs)
        total = total + came.astype(F32)
    weight_part = (total[:share] / (SIDE * SIDE * SIDE)).reshape(1, share, 2, half)
    return (jnp.where(is_decoder, enc_share, in_share)[None], weight_part)


def solution(mesh):
    split = Mesh(mesh.devices.reshape(2, SIDE, SIDE, SIDE, N_MP), ("sec", "x", "zh", "y", "mp"))
    dp = ("x", "zh", "y")
    in_specs = (
        P("sec", dp, None),
        P("sec", None, None, "mp"),
        P(dp, "mp"),
        P(dp, "mp"),
        P("mp", dp),
        P("mp", dp),
        P(dp, None),
    )
    out_specs = (P("sec", (*dp, "mp"), None), P("sec", dp, None, "mp"))
    return jax.shard_map(shards, mesh=split, in_specs=in_specs, out_specs=out_specs, check_vma=False)
```

```python
import jax
import jax.numpy as jnp
from jax import lax
from jax.experimental import pallas as pl
from jax.experimental.pallas import tpu as pltpu
from jax.sharding import Mesh
from jax.sharding import PartitionSpec as P

HEAD_DIM = 128
SPAN = 64
NEIGH = 128
BLOCKS = 4
N_MP = 4
SIDE = 4
PADDED = 16
SCALE = HEAD_DIM ** (-0.5)
F32 = jnp.float32
BF16 = jnp.bfloat16
NT = (((1,), (1,)), ((), ()))
TN = (((0,), (0,)), ((), ()))
VMEM_LIMIT = 12 * 1024 * 1024


def mm(left, right, dims=(((1,), (0,)), ((), ()))):
    return lax.dot_general(left, right, dims, preferred_element_type=F32)


def block_rows(index):
    return pl.ds(pl.multiple_of(index * NEIGH, NEIGH), NEIGH)


def on_section(sec_ref, section):
    return pl.when(sec_ref[0] == section)


def decoder_kernel(mp_ref, span_ref, rows_ref, weight_ref, query_ref, grad_ref, lse_ref, delta_ref,
                   kv_grad_ref, part0, part1, part2, part3, kv_ref, part_ref):
    half = weight_ref.shape[1] // 2
    kv_ref[...] = mm(rows_ref[...], weight_ref[...]).astype(BF16)
    lane = lax.broadcasted_iota(jnp.int32, (1, 2 * SPAN), 1)
    used = []
    for block in range(BLOCKS):
        flags = [
            jnp.where((span_ref[c, 0] == block) | (span_ref[c, 1] == block), 1, 0) for c in range(2)
        ]
        used.append(jnp.where(lane < SPAN, flags[0], flags[1]) > 0)
    for head in range(half // HEAD_DIM):
        lo = head * HEAD_DIM
        query = query_ref[:, lo:lo + HEAD_DIM]
        grad = grad_ref[:, lo:lo + HEAD_DIM]
        lse = lse_ref[head:head + 1, :]
        delta = delta_ref[head:head + 1, :]
        key = kv_ref[:, lo:lo + HEAD_DIM]
        value = kv_ref[:, half + lo:half + lo + HEAD_DIM]
        shift = jnp.concatenate(
            [jnp.broadcast_to(jnp.where(flag, lse, jnp.inf), (NEIGH, 2 * SPAN)) for flag in used], axis=0
        )
        probs = jnp.exp(mm(key, query, NT) * SCALE - shift)
        value_grad = mm(probs.astype(BF16), grad)
        score_grad = probs * (mm(value, grad, NT) - delta)
        key_grad = mm(score_grad.astype(BF16), query) * SCALE
        kv_grad_ref[:, lo:lo + HEAD_DIM] = key_grad.astype(BF16)
        kv_grad_ref[:, half + lo:half + lo + HEAD_DIM] = value_grad.astype(BF16)
    part_ref[...] = mm(kv_grad_ref[...], weight_ref[...], NT).astype(BF16)
    for step, part in enumerate((part0, part1, part2, part3)):
        part[...] = part_ref[block_rows(lax.rem(mp_ref[0] + step, N_MP)), :]


def ordered(rows, order_ref):
    width = order_ref.shape[1]
    place = lax.broadcasted_iota(jnp.int32, (width, width), 0) == order_ref[...]
    return mm(rows, jnp.where(place, 1.0, 0.0).astype(BF16)).astype(BF16)


def store_chunks(out_ref, value, column=0):
    chunk, width = out_ref.shape[1], value.shape[1]
    for index in range(out_ref.shape[0]):
        out_ref[index, :, column:column + width] = value[index * chunk:(index + 1) * chunk, :].astype(BF16)


def decoder_weight_kernel(sec_ref, rows_ref, kv_grad_ref, order_ref, partial_ref):
    @on_section(sec_ref, 0)
    def work():
        store_chunks(partial_ref, mm(ordered(rows_ref[...], order_ref), kv_grad_ref[...], TN))


def prepare_kernel(rows_ref, weight_ref, order_ref, ordered_ref, hidden_ref, slope_ref):
    half = weight_ref.shape[1] // 2
    ordered_ref[...] = ordered(rows_ref[...], order_ref)
    pre = mm(rows_ref[...], weight_ref[:, :half])
    square = pre * pre
    tangent = jnp.tanh(0.7978845608 * (pre + 0.044715 * square * pre))
    hidden_ref[...] = (0.5 * pre * (1.0 + tangent)).astype(BF16)
    slope_ref[...] = 0.5 * (1.0 + tangent) + 0.5 * pre * (1.0 - tangent * tangent) * 0.7978845608 * (
        1.0 + 0.134145 * square
    )


def first_kernel(sec_ref, mp_ref, span_ref, rows_ref, weight_ref, query_ref, grad_ref, lse_ref, delta_ref, order_ref,
                 kv_grad_ref, part0, part1, part2, part3, ordered_ref, hidden_ref, slope_ref, kv_ref, part_ref):
    @on_section(sec_ref, 0)
    def decoder():
        decoder_kernel(
            mp_ref, span_ref, rows_ref, weight_ref, query_ref, grad_ref, lse_ref, delta_ref,
            kv_grad_ref, part0, part1, part2, part3, kv_ref, part_ref,
        )

    @on_section(sec_ref, 1)
    def encoder():
        prepare_kernel(rows_ref, weight_ref, order_ref, ordered_ref, hidden_ref, slope_ref)


def encoder_kernel(sec_ref, mp_ref, order_ref, ordered_ref, weight_ref, hidden_ref, slope_ref, got0, got1, got2, got3,
                   keep_ref, partial_ref, part0, part1, part2, part3, arrived_ref, part_ref):
    del keep_ref
    @on_section(sec_ref, 1)
    def work():
        half = weight_ref.shape[1] // 2
        for step, got in enumerate((got0, got3, got2, got1)):
            arrived_ref[block_rows(lax.rem(mp_ref[0] + step, N_MP)), :] = got[...]
        arrived = arrived_ref[...]
        pre_grad = (mm(arrived, weight_ref[:, half:]) * slope_ref[...]).astype(BF16)
        store_chunks(partial_ref, mm(ordered(arrived, order_ref), hidden_ref[...], TN), half)
        store_chunks(partial_ref, mm(ordered_ref[...], pre_grad, TN))
        part_ref[...] = mm(pre_grad, weight_ref[:, :half], NT).astype(BF16)
        for step, part in enumerate((part0, part1, part2, part3)):
            part[...] = part_ref[block_rows(lax.rem(mp_ref[0] + step, N_MP)), :]


def sum_kernel(zh_ref, piece_ref, out0, out1, out2, out3, total_ref):
    total = piece_ref[0].astype(F32)
    for source in range(1, piece_ref.shape[0]):
        total = total + piece_ref[source].astype(F32)
    count = total.shape[0]
    share = count // SIDE
    total_ref[:count, :] = total
    total_ref[count:, :] = jnp.zeros((total_ref.shape[0] - count, total_ref.shape[1]), F32)
    for block in range(SIDE):
        rows = total_ref[block * share:block * share + PADDED, :].astype(BF16)
        for step, out in enumerate((out0, out1, out2, out3)):
            @pl.when(lax.rem(zh_ref[0] + step, SIDE) == block)
            def store(rows=rows, out=out):
                out[...] = rows


def vmem():
    return pl.BlockSpec(memory_space=pltpu.VMEM)


def smem():
    return pl.BlockSpec(memory_space=pltpu.SMEM)


def call(kernel, outs, args, scalars=0, scratch=(), flops=0, alias=None):
    return pl.pallas_call(
        kernel,
        out_shape=[jax.ShapeDtypeStruct(shape, kind) for shape, kind in outs],
        in_specs=[smem()] * scalars + [vmem()] * (len(args) - scalars),
        out_specs=[vmem()] * len(outs),
        scratch_shapes=list(scratch),
        input_output_aliases=alias or {},
        compiler_params=pltpu.CompilerParams(vmem_limit_bytes=VMEM_LIMIT),
        cost_estimate=pl.CostEstimate(flops=flops, bytes_accessed=4 << 20, transcendentals=0),
    )(*args)


def mp_move(value, source, target, step):
    pairs = [(source * N_MP + m, target * N_MP + (m + step) % N_MP) for m in range(N_MP)]
    return lax.ppermute(value, ("sec", "mp"), pairs)


def mp_parts(parts, source, target):
    moved = [mp_move(parts[step], source, target, step) for step in (2, 1, 3)]
    return moved + [mp_move(parts[0], source, target, 0) if source != target else parts[0]]


def mp_sum(parts):
    total = parts[0].astype(F32)
    for part in parts[1:]:
        total = total + part.astype(F32)
    return total.astype(BF16)


def shards(states, proj_weights, queries, out_grad, logsumexp, delta, span_blocks):
    rows = states[0]
    local_rows, width = rows.shape
    half = proj_weights.shape[3]
    weights = proj_weights[0].reshape(width, 2 * half)
    quarter = local_rows // N_MP
    pieces = SIDE * SIDE
    chunk = width // pieces
    share = chunk // SIDE
    sec = lax.axis_index("sec").astype(jnp.int32).reshape(1)
    mp = lax.axis_index("mp").astype(jnp.int32).reshape(1)
    zh = lax.axis_index("zh").astype(jnp.int32).reshape(1)
    is_decoder = sec[0] == 0
    order = jnp.arange(width, dtype=jnp.int32).reshape(SIDE, SIDE, SIDE, share)
    order = order.transpose(0, 2, 1, 3).reshape(1, width)

    part_outs = [((quarter, width), BF16)] * N_MP
    piece_out = ((pieces, chunk, 2 * half), BF16)
    col_out = ((local_rows, half), BF16)
    part_scratch = pltpu.VMEM((local_rows, width), BF16)
    sum_scratch = pltpu.VMEM((SIDE * PADDED, 2 * half), F32)
    cols_flops = 2 * local_rows * width * half

    ordered_out = ((local_rows, width), BF16)
    kv_grad, *enc_parts, ordered_rows, hidden, slope = call(
        first_kernel,
        [((local_rows, 2 * half), BF16)] + part_outs + [ordered_out, col_out, ((local_rows, half), F32)],
        (sec, mp, span_blocks, rows, weights, queries, out_grad, logsumexp, delta, order),
        scalars=3,
        scratch=[pltpu.VMEM((local_rows, 2 * half), BF16), part_scratch],
        flops=4 * cols_flops,
    )
    with jax.named_scope("enc_reduce"):
        enc_parts = mp_parts(enc_parts, 0, 1)
    enc_share = mp_sum(enc_parts)
    with jax.named_scope("enc_gather"):
        got = {step: mp_move(enc_share, 1, 1, step) for step in (2, 1, 3)}
        got = [enc_share, got[1], got[2], got[3]]
    with jax.named_scope("enc_out"):
        enc_share = lax.ppermute(enc_share, "sec", [(1, 0)])

    (partial,) = call(
        decoder_weight_kernel, [piece_out], (sec, rows, kv_grad, order), scalars=1, flops=4 * cols_flops
    )
    partial, *in_parts = call(
        encoder_kernel,
        [piece_out] + part_outs,
        (sec, mp, order, ordered_rows, weights, hidden, slope, *got, partial),
        scalars=2,
        scratch=[part_scratch] * 2,
        flops=5 * cols_flops,
        alias={11: 0},
    )
    with jax.named_scope("exchange"):
        partial = lax.all_to_all(partial, ("x", "y"), 0, 0, tiled=True)
    with jax.named_scope("in_reduce"):
        in_parts = mp_parts(in_parts, 1, 1)
    in_share = mp_sum(in_parts)
    blocks = call(
        sum_kernel, [((PADDED, 2 * half), BF16)] * SIDE, (zh, partial), scalars=1, scratch=[sum_scratch]
    )
    total = blocks[0].astype(F32)
    for step in range(1, SIDE):
        pairs = [(source, (source + step) % SIDE) for source in range(SIDE)]
        with jax.named_scope("zh_reduce"):
            came = lax.ppermute(blocks[step], "zh", pairs)
        total = total + came.astype(F32)
    weight_part = (total[:share] / (SIDE * SIDE * SIDE)).reshape(1, share, 2, half)
    return (jnp.where(is_decoder, enc_share, in_share)[None], weight_part)


def solution(mesh):
    split = Mesh(mesh.devices.reshape(2, SIDE, SIDE, SIDE, N_MP), ("sec", "x", "zh", "y", "mp"))
    dp = ("x", "zh", "y")
    in_specs = (
        P("sec", dp, None),
        P("sec", None, None, "mp"),
        P(dp, "mp"),
        P(dp, "mp"),
        P("mp", dp),
        P("mp", dp),
        P(dp, None),
    )
    out_specs = (P("sec", (*dp, "mp"), None), P("sec", dp, None, "mp"))
    return jax.shard_map(shards, mesh=split, in_specs=in_specs, out_specs=out_specs, check_vma=False)
```

```python
import jax
import jax.numpy as jnp
from jax import lax
from jax.experimental import pallas as pl
from jax.experimental.pallas import tpu as pltpu
from jax.sharding import Mesh
from jax.sharding import PartitionSpec as P

HEAD_DIM = 128
SPAN = 64
NEIGH = 128
BLOCKS = 4
N_MP = 4
SIDE = 4
PADDED = 16
SCALE = HEAD_DIM ** (-0.5)
F32 = jnp.float32
BF16 = jnp.bfloat16
NT = (((1,), (1,)), ((), ()))
TN = (((0,), (0,)), ((), ()))
VMEM_LIMIT = 12 * 1024 * 1024


def mm(left, right, dims=(((1,), (0,)), ((), ()))):
    return lax.dot_general(left, right, dims, preferred_element_type=F32)


def block_rows(index):
    return pl.ds(pl.multiple_of(index * NEIGH, NEIGH), NEIGH)


def on_section(sec_ref, section):
    return pl.when(sec_ref[0] == section)


def first_kernel(sec_ref, mp_ref, span_ref, rows_ref, weight_ref, query_ref, grad_ref, lse_ref, delta_ref,
                 order_ref, kv_grad_ref, part0, part1, part2, part3, hidden_ref, slope_ref, ordered_ref, kv_ref, part_ref):
    @on_section(sec_ref, 0)
    def decoder():
        decoder_work(
            mp_ref, span_ref, rows_ref, weight_ref, query_ref, grad_ref, lse_ref, delta_ref,
            kv_grad_ref, part0, part1, part2, part3, kv_ref, part_ref,
        )

    @on_section(sec_ref, 1)
    def encoder():
        half = weight_ref.shape[1] // 2
        pre = mm(rows_ref[...], weight_ref[:, :half])
        square = pre * pre
        tangent = jnp.tanh(0.7978845608 * (pre + 0.044715 * square * pre))
        hidden_ref[...] = (0.5 * pre * (1.0 + tangent)).astype(BF16)
        slope_ref[...] = 0.5 * (1.0 + tangent) + 0.5 * pre * (1.0 - tangent * tangent) * 0.7978845608 * (
            1.0 + 0.134145 * square
        )
        place = places(order_ref)
        ordered_ref[...] = mm(rows_ref[...], place).astype(BF16)


def decoder_work(mp_ref, span_ref, rows_ref, weight_ref, query_ref, grad_ref, lse_ref, delta_ref,
                 kv_grad_ref, part0, part1, part2, part3, kv_ref, part_ref):
    half = weight_ref.shape[1] // 2
    kv_ref[...] = mm(rows_ref[...], weight_ref[...]).astype(BF16)
    lane = lax.broadcasted_iota(jnp.int32, (1, 2 * SPAN), 1)
    used = []
    for block in range(BLOCKS):
        flags = [
            jnp.where((span_ref[c, 0] == block) | (span_ref[c, 1] == block), 1, 0) for c in range(2)
        ]
        used.append(jnp.where(lane < SPAN, flags[0], flags[1]) > 0)
    for head in range(half // HEAD_DIM):
        lo = head * HEAD_DIM
        query = query_ref[:, lo:lo + HEAD_DIM]
        grad = grad_ref[:, lo:lo + HEAD_DIM]
        lse = lse_ref[head:head + 1, :]
        delta = delta_ref[head:head + 1, :]
        key = kv_ref[:, lo:lo + HEAD_DIM]
        value = kv_ref[:, half + lo:half + lo + HEAD_DIM]
        shift = jnp.concatenate(
            [jnp.broadcast_to(jnp.where(flag, lse, jnp.inf), (NEIGH, 2 * SPAN)) for flag in used], axis=0
        )
        probs = jnp.exp(mm(key, query, NT) * SCALE - shift)
        value_grad = mm(probs.astype(BF16), grad)
        score_grad = probs * (mm(value, grad, NT) - delta)
        key_grad = mm(score_grad.astype(BF16), query) * SCALE
        kv_grad_ref[:, lo:lo + HEAD_DIM] = key_grad.astype(BF16)
        kv_grad_ref[:, half + lo:half + lo + HEAD_DIM] = value_grad.astype(BF16)
    part_ref[...] = mm(kv_grad_ref[...], weight_ref[...], NT).astype(BF16)
    for step, part in enumerate((part0, part1, part2, part3)):
        part[...] = part_ref[block_rows(lax.rem(mp_ref[0] + step, N_MP)), :]


def places(order_ref):
    width = order_ref.shape[1]
    place = lax.broadcasted_iota(jnp.int32, (width, width), 0) == order_ref[...]
    return jnp.where(place, 1.0, 0.0).astype(BF16)


def store_chunks(out_ref, value, column=0):
    chunk, width = out_ref.shape[1], value.shape[1]
    for index in range(out_ref.shape[0]):
        out_ref[index, :, column:column + width] = value[index * chunk:(index + 1) * chunk, :].astype(BF16)


def middle_kernel(sec_ref, rows_ref, weight_ref, kv_grad_ref, order_ref, partial_ref, down_ref):
    @on_section(sec_ref, 0)
    def decoder():
        rows = mm(rows_ref[...], places(order_ref)).astype(BF16)
        store_chunks(partial_ref, mm(rows, kv_grad_ref[...], TN))

    @on_section(sec_ref, 1)
    def encoder():
        half = weight_ref.shape[1] // 2
        down_ref[...] = mm(places(order_ref), weight_ref[:, half:], TN).astype(BF16)


def share_kernel(sec_ref, order_ref, got0, got1, got2, got3, share_ref, ordered_ref):
    @on_section(sec_ref, 1)
    def work():
        total = got0[...].astype(F32)
        for got in (got1, got2, got3):
            total = total + got[...].astype(F32)
        share = total.astype(BF16)
        share_ref[...] = share
        ordered_ref[...] = mm(share, places(order_ref)).astype(BF16)


def encoder_kernel(sec_ref, mp_ref, ordered_ref, weight_ref, down_ref, hidden_ref, slope_ref, got0, got1, got2, got3, keep_ref,
                   partial_ref, part0, part1, part2, part3, pre_grad_ref, arrived_ref, part_ref):
    del keep_ref
    @on_section(sec_ref, 1)
    def work():
        half = hidden_ref.shape[1]
        for step, got in enumerate((got0, got3, got2, got1)):
            arrived_ref[block_rows(lax.rem(mp_ref[0] + step, N_MP)), :] = got[...]
        arrived = arrived_ref[...]
        store_chunks(partial_ref, mm(arrived, hidden_ref[...], TN), half)
        pre_grad_ref[...] = (mm(arrived, down_ref[...]) * slope_ref[...]).astype(BF16)
        store_chunks(partial_ref, mm(ordered_ref[...], pre_grad_ref[...], TN))
        part_ref[...] = mm(pre_grad_ref[...], weight_ref[:, :half], NT).astype(BF16)
        for step, part in enumerate((part0, part1, part2, part3)):
            part[...] = part_ref[block_rows(lax.rem(mp_ref[0] + step, N_MP)), :]


def sum_kernel(zh_ref, piece_ref, out0, out1, out2, out3, total_ref):
    total = piece_ref[0].astype(F32)
    for source in range(1, piece_ref.shape[0]):
        total = total + piece_ref[source].astype(F32)
    count = total.shape[0]
    share = count // SIDE
    total_ref[:count, :] = total
    total_ref[count:, :] = jnp.zeros((total_ref.shape[0] - count, total_ref.shape[1]), F32)
    for block in range(SIDE):
        rows = total_ref[block * share:block * share + PADDED, :].astype(BF16)
        for step, out in enumerate((out0, out1, out2, out3)):
            @pl.when(lax.rem(zh_ref[0] + step, SIDE) == block)
            def store(rows=rows, out=out):
                out[...] = rows


def vmem():
    return pl.BlockSpec(memory_space=pltpu.VMEM)


def smem():
    return pl.BlockSpec(memory_space=pltpu.SMEM)


def call(kernel, outs, args, scalars=0, scratch=(), flops=0, alias=None):
    return pl.pallas_call(
        kernel,
        out_shape=[jax.ShapeDtypeStruct(shape, kind) for shape, kind in outs],
        in_specs=[smem()] * scalars + [vmem()] * (len(args) - scalars),
        out_specs=[vmem()] * len(outs),
        scratch_shapes=list(scratch),
        input_output_aliases=alias or {},
        compiler_params=pltpu.CompilerParams(vmem_limit_bytes=VMEM_LIMIT),
        cost_estimate=pl.CostEstimate(flops=flops, bytes_accessed=4 << 20, transcendentals=0),
    )(*args)


def mp_move(value, source, target, step):
    pairs = [(source * N_MP + m, target * N_MP + (m + step) % N_MP) for m in range(N_MP)]
    return lax.ppermute(value, ("sec", "mp"), pairs)


def mp_parts(parts, source, target):
    moved = [mp_move(parts[step], source, target, step) for step in (2, 1, 3)]
    return moved + [mp_move(parts[0], source, target, 0) if source != target else parts[0]]


def mp_sum(parts):
    total = parts[0].astype(F32)
    for part in parts[1:]:
        total = total + part.astype(F32)
    return total.astype(BF16)


def shards(states, proj_weights, queries, out_grad, logsumexp, delta, span_blocks):
    rows = states[0]
    local_rows, width = rows.shape
    half = proj_weights.shape[3]
    weights = proj_weights[0].reshape(width, 2 * half)
    quarter = local_rows // N_MP
    pieces = SIDE * SIDE
    chunk = width // pieces
    share = chunk // SIDE
    sec = lax.axis_index("sec").astype(jnp.int32).reshape(1)
    mp = lax.axis_index("mp").astype(jnp.int32).reshape(1)
    zh = lax.axis_index("zh").astype(jnp.int32).reshape(1)
    is_decoder = sec[0] == 0
    order = jnp.arange(width, dtype=jnp.int32).reshape(SIDE, SIDE, SIDE, share)
    order = order.transpose(0, 2, 1, 3).reshape(1, width)

    part_outs = [((quarter, width), BF16)] * N_MP
    piece_out = ((pieces, chunk, 2 * half), BF16)
    col_out = ((local_rows, half), BF16)
    part_scratch = pltpu.VMEM((local_rows, width), BF16)
    sum_scratch = pltpu.VMEM((SIDE * PADDED, 2 * half), F32)
    cols_flops = 2 * local_rows * width * half

    ordered_out = ((local_rows, width), BF16)
    kv_grad, *enc_parts, hidden, slope, ordered_rows = call(
        first_kernel,
        [((local_rows, 2 * half), BF16)] + part_outs + [col_out, ((local_rows, half), F32), ordered_out],
        (sec, mp, span_blocks, rows, weights, queries, out_grad, logsumexp, delta, order),
        scalars=3,
        scratch=[pltpu.VMEM((local_rows, 2 * half), BF16), part_scratch],
        flops=4 * cols_flops,
    )
    partial, down = call(
        middle_kernel,
        [piece_out, ((width, half), BF16)],
        (sec, rows, weights, kv_grad, order),
        scalars=1,
        flops=6 * cols_flops,
    )
    with jax.named_scope("enc_reduce"):
        enc_parts = mp_parts(enc_parts, 0, 1)
    enc_share, ordered_share = call(
        share_kernel,
        [((quarter, width), BF16)] * 2,
        (sec, order, *enc_parts),
        scalars=1,
        flops=2 * quarter * width * width,
    )
    with jax.named_scope("enc_gather"):
        got = {step: mp_move(ordered_share, 1, 1, step) for step in (2, 1, 3)}
        got = [ordered_share, got[1], got[2], got[3]]
    with jax.named_scope("enc_out"):
        enc_share = lax.ppermute(enc_share, "sec", [(1, 0)])

    partial, *in_parts = call(
        encoder_kernel,
        [piece_out] + part_outs,
        (sec, mp, ordered_rows, weights, down, hidden, slope, *got, partial),
        scalars=2,
        scratch=[pltpu.VMEM((local_rows, half), BF16), part_scratch, part_scratch],
        flops=4 * cols_flops,
        alias={11: 0},
    )
    with jax.named_scope("exchange"):
        partial = lax.all_to_all(partial, ("x", "y"), 0, 0, tiled=True)
    with jax.named_scope("in_reduce"):
        in_share = mp_sum(mp_parts(in_parts, 1, 1))
    blocks = call(
        sum_kernel, [((PADDED, 2 * half), BF16)] * SIDE, (zh, partial), scalars=1, scratch=[sum_scratch]
    )
    total = blocks[0].astype(F32)
    for step in range(1, SIDE):
        pairs = [(source, (source + step) % SIDE) for source in range(SIDE)]
        with jax.named_scope("zh_reduce"):
            came = lax.ppermute(blocks[step], "zh", pairs)
        total = total + came.astype(F32)
    weight_part = (total[:share] / (SIDE * SIDE * SIDE)).reshape(1, share, 2, half)
    return (jnp.where(is_decoder, enc_share, in_share)[None], weight_part)


def solution(mesh):
    split = Mesh(mesh.devices.reshape(2, SIDE, SIDE, SIDE, N_MP), ("sec", "x", "zh", "y", "mp"))
    dp = ("x", "zh", "y")
    in_specs = (
        P("sec", dp, None),
        P("sec", None, None, "mp"),
        P(dp, "mp"),
        P(dp, "mp"),
        P("mp", dp),
        P("mp", dp),
        P(dp, None),
    )
    out_specs = (P("sec", (*dp, "mp"), None), P("sec", dp, None, "mp"))
    return jax.shard_map(shards, mesh=split, in_specs=in_specs, out_specs=out_specs, check_vma=False)
```

```python
import jax
import jax.numpy as jnp
from jax import lax
from jax.experimental import pallas as pl
from jax.experimental.pallas import tpu as pltpu
from jax.sharding import Mesh
from jax.sharding import PartitionSpec as P

HEAD_DIM = 128
SPAN = 64
NEIGH = 128
BLOCKS = 4
N_MP = 4
OUTER = (0, 3)
INNER = (1, 2)
SIDE = 4
PADDED = 16
SCALE = HEAD_DIM ** (-0.5)
F32 = jnp.float32
BF16 = jnp.bfloat16
NT = (((1,), (1,)), ((), ()))
TN = (((0,), (0,)), ((), ()))
VMEM_LIMIT = 12 * 1024 * 1024


def mm(left, right, dims=(((1,), (0,)), ((), ()))):
    return lax.dot_general(left, right, dims, preferred_element_type=F32)


def block_rows(index):
    return pl.ds(pl.multiple_of(index * NEIGH, NEIGH), NEIGH)


def on_section(sec_ref, section):
    return pl.when(sec_ref[0] == section)


def first_kernel(sec_ref, mp_ref, span_ref, rows_ref, weight_ref, query_ref, grad_ref, lse_ref, delta_ref,
                 order_ref, kv_grad_ref, part0, part1, part2, part3, hidden_ref, slope_ref, ordered_ref, kv_ref, part_ref):
    @on_section(sec_ref, 0)
    def decoder():
        decoder_work(
            mp_ref, span_ref, rows_ref, weight_ref, query_ref, grad_ref, lse_ref, delta_ref,
            kv_grad_ref, part0, part1, part2, part3, kv_ref, part_ref,
        )

    @on_section(sec_ref, 1)
    def encoder():
        half = weight_ref.shape[1] // 2
        pre = mm(rows_ref[...], weight_ref[:, :half])
        square = pre * pre
        tangent = jnp.tanh(0.7978845608 * (pre + 0.044715 * square * pre))
        hidden_ref[...] = (0.5 * pre * (1.0 + tangent)).astype(BF16)
        slope_ref[...] = 0.5 * (1.0 + tangent) + 0.5 * pre * (1.0 - tangent * tangent) * 0.7978845608 * (
            1.0 + 0.134145 * square
        )
        place = places(order_ref)
        ordered_ref[...] = mm(rows_ref[...], place).astype(BF16)


def decoder_work(mp_ref, span_ref, rows_ref, weight_ref, query_ref, grad_ref, lse_ref, delta_ref,
                 kv_grad_ref, part0, part1, part2, part3, kv_ref, part_ref):
    half = weight_ref.shape[1] // 2
    kv_ref[...] = mm(rows_ref[...], weight_ref[...]).astype(BF16)
    lane = lax.broadcasted_iota(jnp.int32, (1, 2 * SPAN), 1)
    used = []
    for block in range(BLOCKS):
        flags = [
            jnp.where((span_ref[c, 0] == block) | (span_ref[c, 1] == block), 1, 0) for c in range(2)
        ]
        used.append(jnp.where(lane < SPAN, flags[0], flags[1]) > 0)
    for head in range(half // HEAD_DIM):
        lo = head * HEAD_DIM
        query = query_ref[:, lo:lo + HEAD_DIM]
        grad = grad_ref[:, lo:lo + HEAD_DIM]
        lse = lse_ref[head:head + 1, :]
        delta = delta_ref[head:head + 1, :]
        key = kv_ref[:, lo:lo + HEAD_DIM]
        value = kv_ref[:, half + lo:half + lo + HEAD_DIM]
        shift = jnp.concatenate(
            [jnp.broadcast_to(jnp.where(flag, lse, jnp.inf), (NEIGH, 2 * SPAN)) for flag in used], axis=0
        )
        probs = jnp.exp(mm(key, query, NT) * SCALE - shift)
        value_grad = mm(probs.astype(BF16), grad)
        score_grad = probs * (mm(value, grad, NT) - delta)
        key_grad = mm(score_grad.astype(BF16), query) * SCALE
        kv_grad_ref[:, lo:lo + HEAD_DIM] = key_grad.astype(BF16)
        kv_grad_ref[:, half + lo:half + lo + HEAD_DIM] = value_grad.astype(BF16)
    part_ref[...] = mm(kv_grad_ref[...], weight_ref[...], NT).astype(BF16)
    for step, part in enumerate((part0, part1, part2, part3)):
        part[...] = part_ref[block_rows(lax.rem(mp_ref[0] + step, N_MP)), :]


def places(order_ref):
    width = order_ref.shape[1]
    place = lax.broadcasted_iota(jnp.int32, (width, width), 0) == order_ref[...]
    return jnp.where(place, 1.0, 0.0).astype(BF16)


def store_chunks(out_ref, value, column=0):
    chunk, width = out_ref.shape[1], value.shape[1]
    for index in range(out_ref.shape[0]):
        out_ref[index, :, column:column + width] = value[index * chunk:(index + 1) * chunk, :].astype(BF16)


def middle_kernel(sec_ref, rows_ref, weight_ref, kv_grad_ref, order_ref, partial_ref, down_ref):
    @on_section(sec_ref, 0)
    def decoder():
        rows = mm(rows_ref[...], places(order_ref)).astype(BF16)
        store_chunks(partial_ref, mm(rows, kv_grad_ref[...], TN))

    @on_section(sec_ref, 1)
    def encoder():
        half = weight_ref.shape[1] // 2
        down_ref[...] = mm(places(order_ref), weight_ref[:, half:], TN).astype(BF16)


def share_kernel(sec_ref, order_ref, got0, got1, got2, got3, share_ref, ordered_ref):
    @on_section(sec_ref, 1)
    def work():
        total = got0[...].astype(F32)
        for got in (got1, got2, got3):
            total = total + got[...].astype(F32)
        share = total.astype(BF16)
        share_ref[...] = share
        ordered_ref[...] = mm(share, places(order_ref)).astype(BF16)


def encoder_kernel(sec_ref, mp_ref, ordered_ref, weight_ref, down_ref, hidden_ref, slope_ref, got0, got1, got2, got3, keep_ref,
                   partial_ref, part0, part1, part2, part3, pre_grad_ref, arrived_ref, part_ref):
    del keep_ref
    @on_section(sec_ref, 1)
    def work():
        half = hidden_ref.shape[1]
        for step, got in enumerate((got0, got3, got2, got1)):
            arrived_ref[block_rows(lax.rem(mp_ref[0] + step, N_MP)), :] = got[...]
        arrived = arrived_ref[...]
        store_chunks(partial_ref, mm(arrived, hidden_ref[...], TN), half)
        pre_grad_ref[...] = (mm(arrived, down_ref[...]) * slope_ref[...]).astype(BF16)
        store_chunks(partial_ref, mm(ordered_ref[...], pre_grad_ref[...], TN))
        part_ref[...] = mm(pre_grad_ref[...], weight_ref[:, :half], NT).astype(BF16)
        for step, part in enumerate((part0, part1, part2, part3)):
            part[...] = part_ref[block_rows(lax.rem(mp_ref[0] + step, N_MP)), :]


def sum_kernel(zh_ref, piece_ref, keep_ref, send_ref, total_ref):
    total = piece_ref[0].astype(F32)
    for source in range(1, piece_ref.shape[0]):
        total = total + piece_ref[source].astype(F32)
    count = total.shape[0]
    share = count // SIDE
    total_ref[:count, :] = total
    total_ref[count:, :] = jnp.zeros((total_ref.shape[0] - count, total_ref.shape[1]), F32)
    inner = (zh_ref[0] == 1) | (zh_ref[0] == 2)

    def put(out_ref, blocks):
        for index, block in enumerate(blocks):
            rows = total_ref[block * share:block * share + PADDED, :]
            out_ref[index * PADDED:(index + 1) * PADDED, :] = rows.astype(out_ref.dtype)

    @pl.when(inner)
    def inner_side():
        put(keep_ref, INNER)
        put(send_ref, OUTER)

    @pl.when(jnp.logical_not(inner))
    def outer_side():
        put(keep_ref, OUTER)
        put(send_ref, INNER)


def halve_kernel(zh_ref, keep_ref, came_ref, own_ref, send_ref):
    upper = zh_ref[0] >= 2
    total = keep_ref[...] + came_ref[...].astype(F32)
    lower_block, upper_block = total[:PADDED, :], total[PADDED:, :]
    own_ref[...] = jnp.where(upper, upper_block, lower_block)
    send_ref[...] = jnp.where(upper, lower_block, upper_block).astype(BF16)


def vmem():
    return pl.BlockSpec(memory_space=pltpu.VMEM)


def smem():
    return pl.BlockSpec(memory_space=pltpu.SMEM)


def call(kernel, outs, args, scalars=0, scratch=(), flops=0, alias=None):
    return pl.pallas_call(
        kernel,
        out_shape=[jax.ShapeDtypeStruct(shape, kind) for shape, kind in outs],
        in_specs=[smem()] * scalars + [vmem()] * (len(args) - scalars),
        out_specs=[vmem()] * len(outs),
        scratch_shapes=list(scratch),
        input_output_aliases=alias or {},
        compiler_params=pltpu.CompilerParams(vmem_limit_bytes=VMEM_LIMIT),
        cost_estimate=pl.CostEstimate(flops=flops, bytes_accessed=4 << 20, transcendentals=0),
    )(*args)


def mp_move(value, source, target, step):
    pairs = [(source * N_MP + m, target * N_MP + (m + step) % N_MP) for m in range(N_MP)]
    return lax.ppermute(value, ("sec", "mp"), pairs)


def mp_parts(parts, source, target):
    moved = [mp_move(parts[step], source, target, step) for step in (2, 1, 3)]
    return moved + [mp_move(parts[0], source, target, 0) if source != target else parts[0]]


def mp_sum(parts):
    total = parts[0].astype(F32)
    for part in parts[1:]:
        total = total + part.astype(F32)
    return total.astype(BF16)


def shards(states, proj_weights, queries, out_grad, logsumexp, delta, span_blocks):
    rows = states[0]
    local_rows, width = rows.shape
    half = proj_weights.shape[3]
    weights = proj_weights[0].reshape(width, 2 * half)
    quarter = local_rows // N_MP
    pieces = SIDE * SIDE
    chunk = width // pieces
    share = chunk // SIDE
    sec = lax.axis_index("sec").astype(jnp.int32).reshape(1)
    mp = lax.axis_index("mp").astype(jnp.int32).reshape(1)
    zh = lax.axis_index("zh").astype(jnp.int32).reshape(1)
    is_decoder = sec[0] == 0
    order = jnp.arange(width, dtype=jnp.int32).reshape(SIDE, SIDE, SIDE, share)
    order = order.transpose(0, 2, 1, 3).reshape(1, width)

    part_outs = [((quarter, width), BF16)] * N_MP
    piece_out = ((pieces, chunk, 2 * half), BF16)
    col_out = ((local_rows, half), BF16)
    part_scratch = pltpu.VMEM((local_rows, width), BF16)
    sum_scratch = pltpu.VMEM((SIDE * PADDED, 2 * half), F32)
    cols_flops = 2 * local_rows * width * half

    ordered_out = ((local_rows, width), BF16)
    kv_grad, *enc_parts, hidden, slope, ordered_rows = call(
        first_kernel,
        [((local_rows, 2 * half), BF16)] + part_outs + [col_out, ((local_rows, half), F32), ordered_out],
        (sec, mp, span_blocks, rows, weights, queries, out_grad, logsumexp, delta, order),
        scalars=3,
        scratch=[pltpu.VMEM((local_rows, 2 * half), BF16), part_scratch],
        flops=4 * cols_flops,
    )
    partial, down = call(
        middle_kernel,
        [piece_out, ((width, half), BF16)],
        (sec, rows, weights, kv_grad, order),
        scalars=1,
        flops=6 * cols_flops,
    )
    with jax.named_scope("enc_reduce"):
        enc_parts = mp_parts(enc_parts, 0, 1)
    enc_share, ordered_share = call(
        share_kernel,
        [((quarter, width), BF16)] * 2,
        (sec, order, *enc_parts),
        scalars=1,
        flops=2 * quarter * width * width,
    )
    with jax.named_scope("enc_gather"):
        got = {step: mp_move(ordered_share, 1, 1, step) for step in (2, 1, 3)}
        got = [ordered_share, got[1], got[2], got[3]]
    with jax.named_scope("enc_out"):
        enc_share = lax.ppermute(enc_share, "sec", [(1, 0)])

    partial, *in_parts = call(
        encoder_kernel,
        [piece_out] + part_outs,
        (sec, mp, ordered_rows, weights, down, hidden, slope, *got, partial),
        scalars=2,
        scratch=[pltpu.VMEM((local_rows, half), BF16), part_scratch, part_scratch],
        flops=4 * cols_flops,
        alias={11: 0},
    )
    with jax.named_scope("exchange"):
        partial = lax.all_to_all(partial, ("x", "y"), 0, 0, tiled=True)
    with jax.named_scope("in_reduce"):
        in_share = mp_sum(mp_parts(in_parts, 1, 1))
    block_shape = (PADDED, 2 * half)
    pair_shape = (2 * PADDED, 2 * half)
    keep, send = call(sum_kernel, [(pair_shape, F32), (pair_shape, BF16)], (zh, partial), scalars=1, scratch=[sum_scratch])
    with jax.named_scope("zh_first"):
        came = lax.ppermute(send, "zh", [(0, 1), (1, 0), (2, 3), (3, 2)])
    own, send = call(halve_kernel, [(block_shape, F32), (block_shape, BF16)], (zh, keep, came), scalars=1)
    with jax.named_scope("zh_second"):
        came = lax.ppermute(send, "zh", [(0, 3), (3, 0), (1, 2), (2, 1)])
    total = own + came.astype(F32)
    weight_part = (total[:share] / (SIDE * SIDE * SIDE)).reshape(1, share, 2, half)
    return (jnp.where(is_decoder, enc_share, in_share)[None], weight_part)


def solution(mesh):
    split = Mesh(mesh.devices.reshape(2, SIDE, SIDE, SIDE, N_MP), ("sec", "x", "zh", "y", "mp"))
    dp = ("x", "zh", "y")
    in_specs = (
        P("sec", dp, None),
        P("sec", None, None, "mp"),
        P(dp, "mp"),
        P(dp, "mp"),
        P("mp", dp),
        P("mp", dp),
        P(dp, None),
    )
    out_specs = (P("sec", (*dp, "mp"), None), P("sec", dp, None, "mp"))
    return jax.shard_map(shards, mesh=split, in_specs=in_specs, out_specs=out_specs, check_vma=False)
```

```python
import jax
import jax.numpy as jnp
from jax import lax
from jax.experimental import pallas as pl
from jax.experimental.pallas import tpu as pltpu
from jax.sharding import Mesh
from jax.sharding import PartitionSpec as P

HEAD_DIM = 128
SPAN = 64
NEIGH = 128
BLOCKS = 4
N_MP = 4
OUTER = (0, 3)
INNER = (1, 2)
SIDE = 4
PADDED = 16
SCALE = HEAD_DIM ** (-0.5)
F32 = jnp.float32
BF16 = jnp.bfloat16
NT = (((1,), (1,)), ((), ()))
TN = (((0,), (0,)), ((), ()))
VMEM_LIMIT = 12 * 1024 * 1024


def mm(left, right, dims=(((1,), (0,)), ((), ()))):
    return lax.dot_general(left, right, dims, preferred_element_type=F32)


def block_rows(index):
    return pl.ds(pl.multiple_of(index * NEIGH, NEIGH), NEIGH)


def on_section(sec_ref, section):
    return pl.when(sec_ref[0] == section)


def first_kernel(sec_ref, mp_ref, span_ref, rows_ref, weight_ref, query_ref, grad_ref, lse_ref, delta_ref,
                 order_ref, kv_grad_ref, part0, part1, part2, part3, hidden_ref, slope_ref, ordered_ref, kv_ref, part_ref):
    @on_section(sec_ref, 0)
    def decoder():
        decoder_work(
            mp_ref, span_ref, rows_ref, weight_ref, query_ref, grad_ref, lse_ref, delta_ref,
            kv_grad_ref, part0, part1, part2, part3, kv_ref, part_ref,
        )

    @on_section(sec_ref, 1)
    def encoder():
        half = weight_ref.shape[1] // 2
        pre = mm(rows_ref[...], weight_ref[:, :half])
        square = pre * pre
        tangent = jnp.tanh(0.7978845608 * (pre + 0.044715 * square * pre))
        hidden_ref[...] = (0.5 * pre * (1.0 + tangent)).astype(BF16)
        slope_ref[...] = 0.5 * (1.0 + tangent) + 0.5 * pre * (1.0 - tangent * tangent) * 0.7978845608 * (
            1.0 + 0.134145 * square
        )
        place = places(order_ref)
        ordered_ref[...] = mm(rows_ref[...], place).astype(BF16)


def decoder_work(mp_ref, span_ref, rows_ref, weight_ref, query_ref, grad_ref, lse_ref, delta_ref,
                 kv_grad_ref, part0, part1, part2, part3, kv_ref, part_ref):
    half = weight_ref.shape[1] // 2
    kv_ref[...] = mm(rows_ref[...], weight_ref[...]).astype(BF16)
    lane = lax.broadcasted_iota(jnp.int32, (1, 2 * SPAN), 1)
    used = []
    for block in range(BLOCKS):
        flags = [
            jnp.where((span_ref[c, 0] == block) | (span_ref[c, 1] == block), 1, 0) for c in range(2)
        ]
        used.append(jnp.where(lane < SPAN, flags[0], flags[1]) > 0)
    for head in range(half // HEAD_DIM):
        lo = head * HEAD_DIM
        query = query_ref[:, lo:lo + HEAD_DIM]
        grad = grad_ref[:, lo:lo + HEAD_DIM]
        lse = lse_ref[head:head + 1, :]
        delta = delta_ref[head:head + 1, :]
        key = kv_ref[:, lo:lo + HEAD_DIM]
        value = kv_ref[:, half + lo:half + lo + HEAD_DIM]
        shift = jnp.concatenate(
            [jnp.broadcast_to(jnp.where(flag, lse, jnp.inf), (NEIGH, 2 * SPAN)) for flag in used], axis=0
        )
        probs = jnp.exp(mm(key, query, NT) * SCALE - shift)
        value_grad = mm(probs.astype(BF16), grad)
        score_grad = probs * (mm(value, grad, NT) - delta)
        key_grad = mm(score_grad.astype(BF16), query) * SCALE
        kv_grad_ref[:, lo:lo + HEAD_DIM] = key_grad.astype(BF16)
        kv_grad_ref[:, half + lo:half + lo + HEAD_DIM] = value_grad.astype(BF16)
    part_ref[...] = mm(kv_grad_ref[...], weight_ref[...], NT).astype(BF16)
    for step, part in enumerate((part0, part1, part2, part3)):
        part[...] = part_ref[block_rows(lax.rem(mp_ref[0] + step, N_MP)), :]


def places(order_ref):
    width = order_ref.shape[1]
    place = lax.broadcasted_iota(jnp.int32, (width, width), 0) == order_ref[...]
    return jnp.where(place, 1.0, 0.0).astype(BF16)


def store_chunks(out_ref, value, column=0):
    chunk, width = out_ref.shape[1], value.shape[1]
    for index in range(out_ref.shape[0]):
        out_ref[index, :, column:column + width] = value[index * chunk:(index + 1) * chunk, :].astype(BF16)


def middle_kernel(sec_ref, rows_ref, weight_ref, kv_grad_ref, order_ref, partial_ref, down_ref):
    @on_section(sec_ref, 0)
    def decoder():
        rows = mm(rows_ref[...], places(order_ref)).astype(BF16)
        store_chunks(partial_ref, mm(rows, kv_grad_ref[...], TN))

    @on_section(sec_ref, 1)
    def encoder():
        half = weight_ref.shape[1] // 2
        down_ref[...] = mm(places(order_ref), weight_ref[:, half:], TN).astype(BF16)


def share_kernel(sec_ref, order_ref, got0, got1, got2, got3, share_ref, ordered_ref):
    @on_section(sec_ref, 1)
    def work():
        total = got0[...].astype(F32)
        for got in (got1, got2, got3):
            total = total + got[...].astype(F32)
        share = total.astype(BF16)
        share_ref[...] = share
        ordered_ref[...] = mm(share, places(order_ref)).astype(BF16)


def encoder_kernel(sec_ref, mp_ref, ordered_ref, down_ref, hidden_ref, slope_ref, got0, got1, got2, got3, keep_ref,
                   partial_ref, pre_grad_ref, arrived_ref):
    del keep_ref
    @on_section(sec_ref, 1)
    def work():
        half = hidden_ref.shape[1]
        for step, got in enumerate((got0, got3, got2, got1)):
            arrived_ref[block_rows(lax.rem(mp_ref[0] + step, N_MP)), :] = got[...]
        arrived = arrived_ref[...]
        store_chunks(partial_ref, mm(arrived, hidden_ref[...], TN), half)
        pre_grad_ref[...] = (mm(arrived, down_ref[...]) * slope_ref[...]).astype(BF16)
        store_chunks(partial_ref, mm(ordered_ref[...], pre_grad_ref[...], TN))


def input_kernel(sec_ref, mp_ref, weight_ref, pre_grad_ref, part0, part1, part2, part3, part_ref):
    @on_section(sec_ref, 1)
    def work():
        half = pre_grad_ref.shape[1]
        part_ref[...] = mm(pre_grad_ref[...], weight_ref[:, :half], NT).astype(BF16)
        for step, part in enumerate((part0, part1, part2, part3)):
            part[...] = part_ref[block_rows(lax.rem(mp_ref[0] + step, N_MP)), :]


def sum_kernel(zh_ref, piece_ref, keep_ref, send_ref, total_ref):
    total = piece_ref[0].astype(F32)
    for source in range(1, piece_ref.shape[0]):
        total = total + piece_ref[source].astype(F32)
    count = total.shape[0]
    share = count // SIDE
    total_ref[:count, :] = total
    total_ref[count:, :] = jnp.zeros((total_ref.shape[0] - count, total_ref.shape[1]), F32)
    inner = (zh_ref[0] == 1) | (zh_ref[0] == 2)

    def put(out_ref, blocks):
        for index, block in enumerate(blocks):
            rows = total_ref[block * share:block * share + PADDED, :]
            out_ref[index * PADDED:(index + 1) * PADDED, :] = rows.astype(out_ref.dtype)

    @pl.when(inner)
    def inner_side():
        put(keep_ref, INNER)
        put(send_ref, OUTER)

    @pl.when(jnp.logical_not(inner))
    def outer_side():
        put(keep_ref, OUTER)
        put(send_ref, INNER)


def halve_kernel(zh_ref, keep_ref, came_ref, own_ref, send_ref):
    upper = zh_ref[0] >= 2
    total = keep_ref[...] + came_ref[...].astype(F32)
    lower_block, upper_block = total[:PADDED, :], total[PADDED:, :]
    own_ref[...] = jnp.where(upper, upper_block, lower_block)
    send_ref[...] = jnp.where(upper, lower_block, upper_block).astype(BF16)


def last_kernel(own_ref, came_ref, out_ref):
    share, half = out_ref.shape[1], out_ref.shape[3]
    total = (own_ref[...] + came_ref[...].astype(F32)) * (1.0 / (SIDE * SIDE * SIDE))
    for column in range(2):
        out_ref[0, :, column, :] = total[:share, column * half:(column + 1) * half]


def vmem():
    return pl.BlockSpec(memory_space=pltpu.VMEM)


def smem():
    return pl.BlockSpec(memory_space=pltpu.SMEM)


def call(kernel, outs, args, scalars=0, scratch=(), flops=0, alias=None):
    return pl.pallas_call(
        kernel,
        out_shape=[jax.ShapeDtypeStruct(shape, kind) for shape, kind in outs],
        in_specs=[smem()] * scalars + [vmem()] * (len(args) - scalars),
        out_specs=[vmem()] * len(outs),
        scratch_shapes=list(scratch),
        input_output_aliases=alias or {},
        compiler_params=pltpu.CompilerParams(vmem_limit_bytes=VMEM_LIMIT),
        cost_estimate=pl.CostEstimate(flops=flops, bytes_accessed=4 << 20, transcendentals=0),
    )(*args)


def mp_move(value, source, target, step):
    pairs = [(source * N_MP + m, target * N_MP + (m + step) % N_MP) for m in range(N_MP)]
    return lax.ppermute(value, ("sec", "mp"), pairs)


def mp_parts(parts, source, target):
    moved = [mp_move(parts[step], source, target, step) for step in (2, 1, 3)]
    return moved + [mp_move(parts[0], source, target, 0) if source != target else parts[0]]


def mp_sum(parts):
    total = parts[0].astype(F32)
    for part in parts[1:]:
        total = total + part.astype(F32)
    return total.astype(BF16)


def shards(states, proj_weights, queries, out_grad, logsumexp, delta, span_blocks):
    rows = states[0]
    local_rows, width = rows.shape
    half = proj_weights.shape[3]
    weights = proj_weights[0].reshape(width, 2 * half)
    quarter = local_rows // N_MP
    pieces = SIDE * SIDE
    chunk = width // pieces
    share = chunk // SIDE
    sec = lax.axis_index("sec").astype(jnp.int32).reshape(1)
    mp = lax.axis_index("mp").astype(jnp.int32).reshape(1)
    zh = lax.axis_index("zh").astype(jnp.int32).reshape(1)
    is_decoder = sec[0] == 0
    order = jnp.arange(width, dtype=jnp.int32).reshape(SIDE, SIDE, SIDE, share)
    order = order.transpose(0, 2, 1, 3).reshape(1, width)

    part_outs = [((quarter, width), BF16)] * N_MP
    piece_out = ((pieces, chunk, 2 * half), BF16)
    col_out = ((local_rows, half), BF16)
    part_scratch = pltpu.VMEM((local_rows, width), BF16)
    sum_scratch = pltpu.VMEM((SIDE * PADDED, 2 * half), F32)
    cols_flops = 2 * local_rows * width * half

    ordered_out = ((local_rows, width), BF16)
    kv_grad, *enc_parts, hidden, slope, ordered_rows = call(
        first_kernel,
        [((local_rows, 2 * half), BF16)] + part_outs + [col_out, ((local_rows, half), F32), ordered_out],
        (sec, mp, span_blocks, rows, weights, queries, out_grad, logsumexp, delta, order),
        scalars=3,
        scratch=[pltpu.VMEM((local_rows, 2 * half), BF16), part_scratch],
        flops=4 * cols_flops,
    )
    partial, down = call(
        middle_kernel,
        [piece_out, ((width, half), BF16)],
        (sec, rows, weights, kv_grad, order),
        scalars=1,
        flops=6 * cols_flops,
    )
    with jax.named_scope("enc_reduce"):
        enc_parts = mp_parts(enc_parts, 0, 1)
    enc_share, ordered_share = call(
        share_kernel,
        [((quarter, width), BF16)] * 2,
        (sec, order, *enc_parts),
        scalars=1,
        flops=2 * quarter * width * width,
    )
    with jax.named_scope("enc_gather"):
        got = {step: mp_move(ordered_share, 1, 1, step) for step in (2, 1, 3)}
        got = [ordered_share, got[1], got[2], got[3]]
    with jax.named_scope("enc_out"):
        enc_share = lax.ppermute(enc_share, "sec", [(1, 0)])

    partial, pre_grad = call(
        encoder_kernel,
        [piece_out, col_out],
        (sec, mp, ordered_rows, down, hidden, slope, *got, partial),
        scalars=2,
        scratch=[part_scratch],
        flops=4 * cols_flops,
        alias={10: 0},
    )
    in_parts = call(
        input_kernel,
        part_outs,
        (sec, mp, weights, pre_grad),
        scalars=2,
        scratch=[part_scratch],
        flops=cols_flops,
    )
    partial, *in_parts = lax.optimization_barrier((partial, *in_parts))
    with jax.named_scope("exchange"):
        partial = lax.all_to_all(partial, ("x", "y"), 0, 0, tiled=True)
    with jax.named_scope("in_reduce"):
        in_share = mp_sum(mp_parts(in_parts, 1, 1))
    block_shape = (PADDED, 2 * half)
    pair_shape = (2 * PADDED, 2 * half)
    keep, send = call(sum_kernel, [(pair_shape, F32), (pair_shape, BF16)], (zh, partial), scalars=1, scratch=[sum_scratch])
    with jax.named_scope("zh_first"):
        came = lax.ppermute(send, "zh", [(0, 1), (1, 0), (2, 3), (3, 2)])
    came, row_part = lax.optimization_barrier((came, jnp.where(is_decoder, enc_share, in_share)[None]))
    own, send = call(halve_kernel, [(block_shape, F32), (block_shape, BF16)], (zh, keep, came), scalars=1)
    with jax.named_scope("zh_second"):
        came = lax.ppermute(send, "zh", [(0, 3), (3, 0), (1, 2), (2, 1)])
    (weight_part,) = call(last_kernel, [((1, share, 2, half), F32)], (own, came))
    return (row_part, weight_part)


def solution(mesh):
    split = Mesh(mesh.devices.reshape(2, SIDE, SIDE, SIDE, N_MP), ("sec", "x", "zh", "y", "mp"))
    dp = ("x", "zh", "y")
    in_specs = (
        P("sec", dp, None),
        P("sec", None, None, "mp"),
        P(dp, "mp"),
        P(dp, "mp"),
        P("mp", dp),
        P("mp", dp),
        P(dp, None),
    )
    out_specs = (P("sec", (*dp, "mp"), None), P("sec", dp, None, "mp"))
    return jax.shard_map(shards, mesh=split, in_specs=in_specs, out_specs=out_specs, check_vma=False)
```

```python
import jax
import jax.numpy as jnp
from jax import lax
from jax.experimental import pallas as pl
from jax.experimental.pallas import tpu as pltpu
from jax.sharding import Mesh
from jax.sharding import PartitionSpec as P

HEAD_DIM = 128
SPAN = 64
NEIGH = 128
BLOCKS = 4
N_MP = 4
EARLY = (0, 2, 3)
OUTER = (0, 3)
INNER = (1, 2)
SIDE = 4
PADDED = 16
SCALE = HEAD_DIM ** (-0.5)
F32 = jnp.float32
BF16 = jnp.bfloat16
NT = (((1,), (1,)), ((), ()))
TN = (((0,), (0,)), ((), ()))
VMEM_LIMIT = 12 * 1024 * 1024


def mm(left, right, dims=(((1,), (0,)), ((), ()))):
    return lax.dot_general(left, right, dims, preferred_element_type=F32)


def block_rows(index):
    return pl.ds(pl.multiple_of(index * NEIGH, NEIGH), NEIGH)


def on_section(sec_ref, section):
    return pl.when(sec_ref[0] == section)


def first_kernel(sec_ref, mp_ref, span_ref, rows_ref, weight_ref, query_ref, grad_ref, lse_ref, delta_ref,
                 order_ref, kv_grad_ref, part0, part1, part2, part3, hidden_ref, slope_ref, ordered_ref, kv_ref, part_ref):
    @on_section(sec_ref, 0)
    def decoder():
        decoder_work(
            mp_ref, span_ref, rows_ref, weight_ref, query_ref, grad_ref, lse_ref, delta_ref,
            kv_grad_ref, part0, part1, part2, part3, kv_ref, part_ref,
        )

    @on_section(sec_ref, 1)
    def encoder():
        half = weight_ref.shape[1] // 2
        pre = mm(rows_ref[...], weight_ref[:, :half])
        square = pre * pre
        tangent = jnp.tanh(0.7978845608 * (pre + 0.044715 * square * pre))
        hidden_ref[...] = (0.5 * pre * (1.0 + tangent)).astype(BF16)
        slope_ref[...] = 0.5 * (1.0 + tangent) + 0.5 * pre * (1.0 - tangent * tangent) * 0.7978845608 * (
            1.0 + 0.134145 * square
        )
        place = places(order_ref)
        ordered_ref[...] = mm(rows_ref[...], place).astype(BF16)


def decoder_work(mp_ref, span_ref, rows_ref, weight_ref, query_ref, grad_ref, lse_ref, delta_ref,
                 kv_grad_ref, part0, part1, part2, part3, kv_ref, part_ref):
    half = weight_ref.shape[1] // 2
    kv_ref[...] = mm(rows_ref[...], weight_ref[...]).astype(BF16)
    lane = lax.broadcasted_iota(jnp.int32, (1, 2 * SPAN), 1)
    used = []
    for block in range(BLOCKS):
        flags = [
            jnp.where((span_ref[c, 0] == block) | (span_ref[c, 1] == block), 1, 0) for c in range(2)
        ]
        used.append(jnp.where(lane < SPAN, flags[0], flags[1]) > 0)
    for head in range(half // HEAD_DIM):
        lo = head * HEAD_DIM
        query = query_ref[:, lo:lo + HEAD_DIM]
        grad = grad_ref[:, lo:lo + HEAD_DIM]
        lse = lse_ref[head:head + 1, :]
        delta = delta_ref[head:head + 1, :]
        key = kv_ref[:, lo:lo + HEAD_DIM]
        value = kv_ref[:, half + lo:half + lo + HEAD_DIM]
        shift = jnp.concatenate(
            [jnp.broadcast_to(jnp.where(flag, lse, jnp.inf), (NEIGH, 2 * SPAN)) for flag in used], axis=0
        )
        probs = jnp.exp(mm(key, query, NT) * SCALE - shift)
        value_grad = mm(probs.astype(BF16), grad)
        score_grad = probs * (mm(value, grad, NT) - delta)
        key_grad = mm(score_grad.astype(BF16), query) * SCALE
        kv_grad_ref[:, lo:lo + HEAD_DIM] = key_grad.astype(BF16)
        kv_grad_ref[:, half + lo:half + lo + HEAD_DIM] = value_grad.astype(BF16)
    part_ref[...] = mm(kv_grad_ref[...], weight_ref[...], NT).astype(BF16)
    for step, part in enumerate((part0, part1, part2, part3)):
        part[...] = part_ref[block_rows(lax.rem(mp_ref[0] + step, N_MP)), :]


def places(order_ref):
    width = order_ref.shape[1]
    place = lax.broadcasted_iota(jnp.int32, (width, width), 0) == order_ref[...]
    return jnp.where(place, 1.0, 0.0).astype(BF16)


def store_chunks(out_ref, value, column=0):
    chunk, width = out_ref.shape[1], value.shape[1]
    for index in range(out_ref.shape[0]):
        out_ref[index, :, column:column + width] = value[index * chunk:(index + 1) * chunk, :].astype(BF16)


def middle_kernel(sec_ref, rows_ref, weight_ref, kv_grad_ref, order_ref, partial_ref, down_ref):
    @on_section(sec_ref, 0)
    def decoder():
        rows = mm(rows_ref[...], places(order_ref)).astype(BF16)
        store_chunks(partial_ref, mm(rows, kv_grad_ref[...], TN))

    @on_section(sec_ref, 1)
    def encoder():
        half = weight_ref.shape[1] // 2
        down_ref[...] = mm(places(order_ref), weight_ref[:, half:], TN).astype(BF16)


def share_kernel(sec_ref, order_ref, got0, got1, got2, got3, share_ref, ordered_ref):
    @on_section(sec_ref, 1)
    def work():
        total = got0[...].astype(F32)
        for got in (got1, got2, got3):
            total = total + got[...].astype(F32)
        share = total.astype(BF16)
        share_ref[...] = share
        ordered_ref[...] = mm(share, places(order_ref)).astype(BF16)


def early_kernel(sec_ref, mp_ref, ordered_ref, down_ref, hidden_ref, slope_ref, got0, got1, got2, sum_ref, pre_grad_ref):
    @on_section(sec_ref, 1)
    def work():
        half = hidden_ref.shape[1]
        blocks = [block_rows(lax.rem(mp_ref[0] + step, N_MP)) for step in EARLY]

        def pick(ref):
            return jnp.concatenate([ref[rows, :] for rows in blocks], axis=0)

        arrived = jnp.concatenate([got0[...], got2[...], got1[...]], axis=0)
        sum_ref[:, half:] = mm(arrived, pick(hidden_ref), TN)
        pre_grad = (mm(arrived, down_ref[...]) * pick(slope_ref)).astype(BF16)
        sum_ref[:, :half] = mm(pick(ordered_ref), pre_grad, TN)
        pre_grad_ref[...] = pre_grad


def late_kernel(sec_ref, mp_ref, ordered_ref, weight_ref, down_ref, hidden_ref, slope_ref, got3, sum_ref, early_ref,
                keep_ref, partial_ref, part0, part1, part2, part3, pre_grad_ref, part_ref, stage0, stage1, sems):
    del keep_ref
    @on_section(sec_ref, 1)
    def work():
        half = hidden_ref.shape[1]
        rows = block_rows(lax.rem(mp_ref[0] + 1, N_MP))
        arrived = got3[...]
        store_chunks(stage1, sum_ref[:, half:] + mm(arrived, hidden_ref[rows, :], TN))
        copy1 = pltpu.make_async_copy(stage1, partial_ref.at[:, :, pl.ds(half, half)], sems.at[1])
        copy1.start()
        pre_grad = (mm(arrived, down_ref[...]) * slope_ref[rows, :]).astype(BF16)
        store_chunks(stage0, sum_ref[:, :half] + mm(ordered_ref[rows, :], pre_grad, TN))
        copy0 = pltpu.make_async_copy(stage0, partial_ref.at[:, :, pl.ds(0, half)], sems.at[0])
        copy0.start()
        pre_grad_ref[rows, :] = pre_grad
        for index, step in enumerate(EARLY):
            block = block_rows(lax.rem(mp_ref[0] + step, N_MP))
            pre_grad_ref[block, :] = early_ref[index * NEIGH:(index + 1) * NEIGH, :]
        part_ref[...] = mm(pre_grad_ref[...], weight_ref[:, :half], NT).astype(BF16)
        for step, part in enumerate((part0, part1, part2, part3)):
            part[...] = part_ref[block_rows(lax.rem(mp_ref[0] + step, N_MP)), :]
        copy1.wait()
        copy0.wait()


def sum_kernel(zh_ref, piece_ref, keep_ref, send_ref, total_ref):
    total = piece_ref[0].astype(F32)
    for source in range(1, piece_ref.shape[0]):
        total = total + piece_ref[source].astype(F32)
    count = total.shape[0]
    share = count // SIDE
    total_ref[:count, :] = total
    total_ref[count:, :] = jnp.zeros((total_ref.shape[0] - count, total_ref.shape[1]), F32)
    inner = (zh_ref[0] == 1) | (zh_ref[0] == 2)

    def put(out_ref, blocks):
        for index, block in enumerate(blocks):
            rows = total_ref[block * share:block * share + PADDED, :]
            out_ref[index * PADDED:(index + 1) * PADDED, :] = rows.astype(out_ref.dtype)

    @pl.when(inner)
    def inner_side():
        put(keep_ref, INNER)
        put(send_ref, OUTER)

    @pl.when(jnp.logical_not(inner))
    def outer_side():
        put(keep_ref, OUTER)
        put(send_ref, INNER)


def halve_kernel(zh_ref, keep_ref, came_ref, own_ref, send_ref):
    upper = zh_ref[0] >= 2
    total = keep_ref[...] + came_ref[...].astype(F32)
    lower_block, upper_block = total[:PADDED, :], total[PADDED:, :]
    own_ref[...] = jnp.where(upper, upper_block, lower_block)
    send_ref[...] = jnp.where(upper, lower_block, upper_block).astype(BF16)


def last_kernel(own_ref, came_ref, out_ref):
    share, half = out_ref.shape[1], out_ref.shape[3]
    total = (own_ref[...] + came_ref[...].astype(F32)) * (1.0 / (SIDE * SIDE * SIDE))
    for column in range(2):
        out_ref[0, :, column, :] = total[:share, column * half:(column + 1) * half]


def vmem():
    return pl.BlockSpec(memory_space=pltpu.VMEM)


def smem():
    return pl.BlockSpec(memory_space=pltpu.SMEM)


def call(kernel, outs, args, scalars=0, scratch=(), flops=0, alias=None, far_in=None, far_out=None):
    far = pl.BlockSpec(memory_space=pl.ANY)
    return pl.pallas_call(
        kernel,
        out_shape=[jax.ShapeDtypeStruct(shape, kind) for shape, kind in outs],
        in_specs=[smem() if i < scalars else far if i == far_in else vmem() for i in range(len(args))],
        out_specs=[far if i == far_out else vmem() for i in range(len(outs))],
        scratch_shapes=list(scratch),
        input_output_aliases=alias or {},
        compiler_params=pltpu.CompilerParams(vmem_limit_bytes=VMEM_LIMIT),
        cost_estimate=pl.CostEstimate(flops=flops, bytes_accessed=4 << 20, transcendentals=0),
    )(*args)


def mp_move(value, source, target, step):
    pairs = [(source * N_MP + m, target * N_MP + (m + step) % N_MP) for m in range(N_MP)]
    return lax.ppermute(value, ("sec", "mp"), pairs)


def mp_parts(parts, source, target):
    moved = [mp_move(parts[step], source, target, step) for step in (2, 1, 3)]
    return moved + [mp_move(parts[0], source, target, 0) if source != target else parts[0]]


def mp_sum(parts):
    total = parts[0].astype(F32)
    for part in parts[1:]:
        total = total + part.astype(F32)
    return total.astype(BF16)


def shards(states, proj_weights, queries, out_grad, logsumexp, delta, span_blocks):
    rows = states[0]
    local_rows, width = rows.shape
    half = proj_weights.shape[3]
    weights = proj_weights[0].reshape(width, 2 * half)
    quarter = local_rows // N_MP
    pieces = SIDE * SIDE
    chunk = width // pieces
    share = chunk // SIDE
    sec = lax.axis_index("sec").astype(jnp.int32).reshape(1)
    mp = lax.axis_index("mp").astype(jnp.int32).reshape(1)
    zh = lax.axis_index("zh").astype(jnp.int32).reshape(1)
    is_decoder = sec[0] == 0
    order = jnp.arange(width, dtype=jnp.int32).reshape(SIDE, SIDE, SIDE, share)
    order = order.transpose(0, 2, 1, 3).reshape(1, width)

    part_outs = [((quarter, width), BF16)] * N_MP
    piece_out = ((pieces, chunk, 2 * half), BF16)
    col_out = ((local_rows, half), BF16)
    part_scratch = pltpu.VMEM((local_rows, width), BF16)
    sum_scratch = pltpu.VMEM((SIDE * PADDED, 2 * half), F32)
    cols_flops = 2 * local_rows * width * half

    ordered_out = ((local_rows, width), BF16)
    kv_grad, *enc_parts, hidden, slope, ordered_rows = call(
        first_kernel,
        [((local_rows, 2 * half), BF16)] + part_outs + [col_out, ((local_rows, half), F32), ordered_out],
        (sec, mp, span_blocks, rows, weights, queries, out_grad, logsumexp, delta, order),
        scalars=3,
        scratch=[pltpu.VMEM((local_rows, 2 * half), BF16), part_scratch],
        flops=4 * cols_flops,
    )
    partial, down = call(
        middle_kernel,
        [piece_out, ((width, half), BF16)],
        (sec, rows, weights, kv_grad, order),
        scalars=1,
        flops=6 * cols_flops,
    )
    with jax.named_scope("enc_reduce"):
        enc_parts = mp_parts(enc_parts, 0, 1)
    enc_share, ordered_share = call(
        share_kernel,
        [((quarter, width), BF16)] * 2,
        (sec, order, *enc_parts),
        scalars=1,
        flops=2 * quarter * width * width,
    )
    with jax.named_scope("enc_gather"):
        got = {step: mp_move(ordered_share, 1, 1, step) for step in (2, 1, 3)}
        got = [ordered_share, got[1], got[2], got[3]]
    with jax.named_scope("enc_out"):
        enc_share = lax.ppermute(enc_share, "sec", [(1, 0)])

    sums, early = call(
        early_kernel,
        [((width, 2 * half), F32), ((3 * quarter, half), BF16)],
        (sec, mp, ordered_rows, down, hidden, slope, *got[:3]),
        scalars=2,
        flops=3 * cols_flops,
    )
    stage = pltpu.VMEM((pieces, chunk, half), BF16)
    partial, *in_parts = call(
        late_kernel,
        [piece_out] + part_outs,
        (sec, mp, ordered_rows, weights, down, hidden, slope, got[3], sums, early, partial),
        scalars=2,
        scratch=[pltpu.VMEM((local_rows, half), BF16), part_scratch, stage, stage, pltpu.SemaphoreType.DMA((2,))],
        flops=2 * cols_flops,
        alias={10: 0},
        far_in=10,
        far_out=0,
    )
    with jax.named_scope("exchange"):
        partial = lax.all_to_all(partial, ("x", "y"), 0, 0, tiled=True)
    with jax.named_scope("in_reduce"):
        in_share = mp_sum(mp_parts(in_parts, 1, 1))
    block_shape = (PADDED, 2 * half)
    pair_shape = (2 * PADDED, 2 * half)
    keep, send = call(sum_kernel, [(pair_shape, F32), (pair_shape, BF16)], (zh, partial), scalars=1, scratch=[sum_scratch])
    with jax.named_scope("zh_first"):
        came = lax.ppermute(send, "zh", [(0, 1), (1, 0), (2, 3), (3, 2)])
    came, row_part = lax.optimization_barrier((came, jnp.where(is_decoder, enc_share, in_share)[None]))
    own, send = call(halve_kernel, [(block_shape, F32), (block_shape, BF16)], (zh, keep, came), scalars=1)
    with jax.named_scope("zh_second"):
        came = lax.ppermute(send, "zh", [(0, 3), (3, 0), (1, 2), (2, 1)])
    (weight_part,) = call(last_kernel, [((1, share, 2, half), F32)], (own, came))
    return (row_part, weight_part)


def solution(mesh):
    split = Mesh(mesh.devices.reshape(2, SIDE, SIDE, SIDE, N_MP), ("sec", "x", "zh", "y", "mp"))
    dp = ("x", "zh", "y")
    in_specs = (
        P("sec", dp, None),
        P("sec", None, None, "mp"),
        P(dp, "mp"),
        P(dp, "mp"),
        P("mp", dp),
        P("mp", dp),
        P(dp, None),
    )
    out_specs = (P("sec", (*dp, "mp"), None), P("sec", dp, None, "mp"))
    return jax.shard_map(shards, mesh=split, in_specs=in_specs, out_specs=out_specs, check_vma=False)
```
